512 devices in a mesh: replica: 32 (over z, core), shard: 16 (over y, x).
Axes of the slice: x: 4, y: 4, z: 16, core: 2. Of those that a mesh axis runs over, the one named last changes fastest.
Arguments:
- context_one: bfloat16 [8192, 5120], P('replica', 'shard'), may hold values from -8 to 8
- cotangent_one: bfloat16 [8192, 5120], P('replica', 'shard'), may hold values from -32 to 32
- context_two: bfloat16 [8192, 5120], P('replica', 'shard'), may hold values from -8 to 8
- cotangent_two: bfloat16 [8192, 5120], P('replica', 'shard'), may hold values from -32 to 32
Outputs:
- combined_one: float32 [5120, 5120], P('shard', 'replica')
- combined_two: float32 [5120, 5120], P('shard', 'replica')
The draws below stay inside these ranges and needn't reach their ends.
All inputs are finite; a program needn't handle non-finite values.
Results may differ from the reference program's by a relative error of at most 0.0047.
Values may be sent and summed in bfloat16 or wider, within the bound.
No kernel may reach another device: no remote copies, remote signals or barrier semaphores. Data moves between devices by JAX's collectives and lax.ppermute only.
A program may use at most 64 MiB of HBM per device.

```python
import jax
import jax.numpy as jnp

D = 5120
TOK_REP = 256
N_REPLICA = 32


def mixed_rows(key, scale, spread):
    base_key, noise_key, share_key, column_key, feature_key = jax.random.split(key, 5)
    base = jax.random.normal(base_key, (TOK_REP, D), jnp.float32)
    noise = jax.random.normal(noise_key, (N_REPLICA, TOK_REP, D), jnp.float32)
    ramp = jnp.arange(N_REPLICA, dtype=jnp.float32) / float(max(N_REPLICA - 1, 1))
    jitter = jax.random.uniform(share_key, (N_REPLICA,), jnp.float32, 0.85, 1.0)
    feature_ramp = jnp.arange(D, dtype=jnp.float32) / float(max(D - 1, 1))
    feature_jitter = jax.random.uniform(feature_key, (D,), jnp.float32, 0.8, 1.0)
    feature_share = (0.1 + 0.9 * feature_ramp) * feature_jitter
    share = ((0.15 + 0.7 * ramp) * jitter)[:, None, None] * feature_share[None, None, :]
    columns = jnp.exp(jax.random.uniform(column_key, (D,), jnp.float32, -spread, spread))
    values = (jnp.sqrt(share) * base[None] + jnp.sqrt(1.0 - share) * noise) * columns * scale
    values = jnp.clip(values, -8.0 * scale, 8.0 * scale)
    return values.reshape(N_REPLICA * TOK_REP, D)


def draw_context_one(key, part):
    key = jax.random.fold_in(key, 11)
    return mixed_rows(key, 1.0, 0.35).astype(jnp.bfloat16)


def draw_cotangent_one(key, part):
    key = jax.random.fold_in(key, 12)
    return mixed_rows(key, 4.0, 0.35).astype(jnp.bfloat16)


def draw_context_two(key, part):
    key = jax.random.fold_in(key, 13)
    return mixed_rows(key, 1.0, 0.35).astype(jnp.bfloat16)


def draw_cotangent_two(key, part):
    key = jax.random.fold_in(key, 14)
    return mixed_rows(key, 4.0, 0.35).astype(jnp.bfloat16)


def setup_inputs(seed: int = 0) -> dict:
    seeds = jax.random.split(jax.random.key(seed), 5)
    context_one = draw_context_one(jax.random.fold_in(seeds[4], 71), 0)
    cotangent_one = draw_cotangent_one(jax.random.fold_in(seeds[4], 71), 0)
    context_two = draw_context_two(jax.random.fold_in(seeds[4], 71), 0)
    cotangent_two = draw_cotangent_two(jax.random.fold_in(seeds[4], 71), 0)
    return dict(context_one=context_one, cotangent_one=cotangent_one, context_two=context_two, cotangent_two=cotangent_two)


EPSILON = 1e-6


def adasum_pair(lower_part, upper_part, final):
    lower_f = lower_part.astype(jnp.float32)
    upper_f = upper_part.astype(jnp.float32)
    inner_sum = jnp.sum(lower_f * upper_f)
    lower_sq = jnp.sum(lower_f * lower_f)
    upper_sq = jnp.sum(upper_f * upper_f)
    coeff_lower = 1.0 - inner_sum / (2.0 * (lower_sq + EPSILON))
    coeff_upper = 1.0 - inner_sum / (2.0 * (upper_sq + EPSILON))
    combined = coeff_lower * lower_f + coeff_upper * upper_f
    if final:
        return combined
    return combined.astype(jnp.bfloat16)


def replica_gradient(context, cotangent, first_index):
    rows_context = context[first_index * TOK_REP:(first_index + 1) * TOK_REP]
    rows_cotangent = cotangent[first_index * TOK_REP:(first_index + 1) * TOK_REP]
    product = jnp.dot(rows_context.T, rows_cotangent, preferred_element_type=jnp.float32)
    return (product / float(TOK_REP)).astype(jnp.bfloat16)


def combine_range(context, cotangent, first_index, span_count, final):
    if span_count == 1:
        return replica_gradient(context, cotangent, first_index)
    half_count = span_count // 2
    lower_part = combine_range(context, cotangent, first_index, half_count, False)
    upper_part = combine_range(context, cotangent, first_index + half_count, half_count, False)
    return adasum_pair(lower_part, upper_part, final)


def reference(context_one, cotangent_one, context_two, cotangent_two):
    combined_one = combine_range(context_one, cotangent_one, 0, N_REPLICA, True)
    combined_two = combine_range(context_two, cotangent_two, 0, N_REPLICA, True)
    return (combined_one, combined_two)
```

```python
import functools

import jax
import jax.numpy as jnp
import numpy as np
from jax import lax
from jax.experimental import pallas as pl
from jax.experimental.pallas import tpu as pltpu
from jax.sharding import PartitionSpec as P

EPSILON = 1e-06
SIDE = 4
MAIN = 128
SHIFTS = (0, 1, -1, 2)


def x_moves(d):
    return [
        (y * SIDE + x, y * SIDE + (x + d) % SIDE) for y in range(SIDE) for x in range(SIDE)
    ]


def y_moves(d):
    return [
        (y * SIDE + x, ((y + d) % SIDE) * SIDE + x) for y in range(SIDE) for x in range(SIDE)
    ]


def gather_pieces(piece):
    half = piece.shape[0] // 2
    along_x, along_y = piece[:half], piece[half:]
    got_x = [lax.ppermute(along_x, "shard", x_moves(d)) for d in SHIFTS[1:]]
    got_y = [lax.ppermute(along_y, "shard", y_moves(d)) for d in SHIFTS[1:]]
    line_x = jnp.stack([along_x] + got_x)
    line_y = jnp.stack([along_y] + got_y)
    line_x, line_y = lax.optimization_barrier((line_x, line_y))
    all_x = [line_x] + [lax.ppermute(line_x, "shard", y_moves(d)) for d in SHIFTS[1:]]
    all_y = [line_y] + [lax.ppermute(line_y, "shard", x_moves(d)) for d in SHIFTS[1:]]
    return all_x, all_y


def piece_offsets(tokens_piece):
    me = lax.axis_index("shard")
    y, x = me // SIDE, me % SIDE
    d = jnp.array(SHIFTS, jnp.int32)
    first, second = d[None, :], d[:, None]
    off_x = ((y - second) % SIDE) * SIDE + (x - first) % SIDE
    off_y = ((y - first) % SIDE) * SIDE + (x - second) % SIDE
    return (jnp.stack([off_x, off_y]) * tokens_piece).astype(jnp.int32).reshape(-1)


def gradient_kernel(reps, rows, rem, inv_tokens, off_ref, ctx_ref, *refs):
    pieces = refs[:8]
    grad_ref, gram_ref, cot_ref, store_ref, acc_ref = refs[8:]
    step = pl.program_id(0)
    steps = pl.num_programs(0)
    tok = pieces[0].shape[2]

    def place(which):
        for second in range(4):
            for first in range(4):
                off = pl.multiple_of(off_ref[which * 16 + second * 4 + first], tok)
                cot_ref[pl.ds(off, tok), :] = pieces[which * 4 + second][first, 0]

    @pl.when(step < steps // 2)
    def _():
        place(0)

    @pl.when(step >= steps // 2)
    def _():
        place(1)

    lane = lax.broadcasted_iota(jnp.int32, (rows, MAIN), 1)
    edge = cot_ref[:, 4 * MAIN :]
    for core in range(2):
        both = []
        for layer in range(2):
            j = 2 * core + layer
            rhs = jnp.concatenate([cot_ref[:, j * MAIN : (j + 1) * MAIN], edge], axis=1)
            lhs = ctx_ref[core, layer * rows : (layer + 1) * rows, :]
            g = jnp.dot(lhs, rhs, preferred_element_type=jnp.float32) * inv_tokens
            main = g[:, :MAIN].astype(jnp.bfloat16)
            grad_ref[layer, core] = main
            store_ref[layer, step * 2 + core] = main.astype(jnp.float32)
            both.append(g[:, MAIN:])
        edges = jnp.where(lane < (2 * core + 1) * rem, both[0], both[1])
        if core:
            edges = pltpu.roll(edges, MAIN - 2 * rem, 1)
        edges = jnp.where(lane < 2 * rem, edges, 0.0).astype(jnp.bfloat16)
        grad_ref[2, core] = edges
        store_ref[2, step * 2 + core] = edges.astype(jnp.float32)

    @pl.when(step == steps - 1)
    def _():
        size = reps * 8
        group = 4
        acc_ref[...] = jnp.zeros_like(acc_ref)
        lane_e = lax.broadcasted_iota(jnp.int32, (size, MAIN), 1)

        def body(i, carry):
            lefts, rights = ([], []), ([], [])
            for u in range(group):
                at = pl.multiple_of((i * group + u) * 8, 8)
                e = store_ref[2, :, pl.ds(at, 8), :].reshape(size, MAIN)
                eb = e.astype(jnp.bfloat16)
                for layer in range(2):
                    m = store_ref[layer, :, pl.ds(at, 8), :].reshape(size, MAIN)
                    m = m.astype(jnp.bfloat16)
                    keep = (lane_e >= layer * rem) & (lane_e < (layer + 1) * rem)
                    ek = jnp.where(keep, e, 0.0).astype(jnp.bfloat16)
                    lefts[layer].extend([m, ek])
                    rights[layer].extend([m, eb])
            for layer in range(2):
                acc_ref[layer] += lax.dot_general(
                    jnp.concatenate(lefts[layer], axis=1),
                    jnp.concatenate(rights[layer], axis=1),
                    (((1,), (1,)), ((), ())),
                    preferred_element_type=jnp.float32,
                )
            return carry

        lax.fori_loop(0, rows // (8 * group), body, 0)
        ri = lax.broadcasted_iota(jnp.int32, (size, size), 0)
        ci = lax.broadcasted_iota(jnp.int32, (size, size), 1)
        si = lax.broadcasted_iota(jnp.int32, (size, 128), 0)
        sj = lax.broadcasted_iota(jnp.int32, (size, 128), 1)
        total = jnp.zeros((16, 128), jnp.float32)
        for layer in range(2):
            z = jnp.where(ri % 8 == ci % 8, acc_ref[layer], 0.0)
            z = jnp.sum(z.reshape(reps, 8, size), axis=1)
            for h in range(2):
                pick = jnp.where(sj == (2 * layer + h) * 32 + si // 8, 1.0, 0.0)
                total += jnp.dot(
                    z[h * 16 : (h + 1) * 16],
                    pick.astype(jnp.float32),
                    precision=lax.Precision.HIGHEST,
                    preferred_element_type=jnp.float32,
                )
        gram_ref[...] = jnp.broadcast_to(total[None], gram_ref.shape)


def gradients(ctx, pieces_x, pieces_y, offsets, shards, tokens):
    reps, rows2, _ = ctx.shape
    rows = rows2 // 2
    rem = (pieces_x[0].shape[-1] - 4 * MAIN) // 4
    steps = reps // 2
    half = steps // 2
    _, _, tok, width = pieces_x[0].shape
    block = (4, 1, tok, width)
    in_specs = [pl.BlockSpec((2, rows2, tokens), lambda i, o: (i, 0, 0))]
    in_specs += [
        pl.BlockSpec(block, lambda i, o: (0, jnp.minimum(i, half - 1), 0, 0))
    ] * 4
    in_specs += [
        pl.BlockSpec(block, lambda i, o: (0, jnp.maximum(i - half, 0), 0, 0))
    ] * 4
    return pl.pallas_call(
        functools.partial(gradient_kernel, reps, rows, rem, 1.0 / tokens),
        grid_spec=pltpu.PrefetchScalarGridSpec(
            num_scalar_prefetch=1,
            grid=(steps,),
            in_specs=in_specs,
            out_specs=[
                pl.BlockSpec((3, 2, rows, MAIN), lambda i, o: (0, i, 0, 0)),
                pl.BlockSpec((shards, 16, 128), lambda i, o: (0, 0, 0)),
            ],
            scratch_shapes=[
                pltpu.VMEM((tokens, width), jnp.bfloat16),
                pltpu.VMEM((3, reps, rows, MAIN), jnp.float32),
                pltpu.VMEM((2, reps * 8, reps * 8), jnp.float32),
            ],
        ),
        out_shape=[
            jax.ShapeDtypeStruct((3, reps, rows, MAIN), jnp.bfloat16),
            jax.ShapeDtypeStruct((shards, 16, 128), jnp.float32),
        ],
        compiler_params=pltpu.CompilerParams(vmem_limit_bytes=48 * 1024 * 1024),
    )(offsets, ctx, *pieces_x, *pieces_y)


def tree_weights(gram):
    n = gram.shape[0]
    ri = lax.broadcasted_iota(jnp.int32, (n, n), 0)
    ci = lax.broadcasted_iota(jnp.int32, (n, n), 1)
    weight = jnp.ones((n, 1), jnp.float32)
    for k in range(n.bit_length() - 1):
        same = (ri >> k) == (ci >> k)
        other = (ri >> k) == ((ci >> k) ^ 1)
        twin = ri == (ci ^ (1 << k))
        own = jnp.where(same, gram, 0.0)
        cross = jnp.where(other, gram, 0.0)
        coeffs = []
        for axis in (1, 0):
            norm = jnp.sum(own, axis=1 - axis, keepdims=True)
            norm = jnp.sum(jnp.where(same, norm, 0.0), axis=axis, keepdims=True)
            inner = jnp.sum(cross, axis=1 - axis, keepdims=True)
            inner = jnp.sum(jnp.where(same, inner, 0.0), axis=axis, keepdims=True)
            coeffs.append((jnp.maximum(norm, 0.0), inner))
        (norm_r, inner_r), (norm_c, inner_c) = coeffs
        twin_r = jnp.sum(jnp.where(twin, norm_c, 0.0), axis=1, keepdims=True)
        twin_c = jnp.sum(jnp.where(twin, norm_r, 0.0), axis=0, keepdims=True)
        cap_r = jnp.sqrt(norm_r) * jnp.sqrt(twin_r)
        cap_c = jnp.sqrt(norm_c) * jnp.sqrt(twin_c)
        inner_r = jnp.clip(inner_r, -cap_r, cap_r)
        inner_c = jnp.clip(inner_c, -cap_c, cap_c)
        coeff_r = 1.0 - inner_r / (2.0 * (norm_r + EPSILON))
        coeff_c = 1.0 - inner_c / (2.0 * (norm_c + EPSILON))
        weight = weight * coeff_r
        gram = gram * coeff_r * coeff_c
    return weight


def combine_kernel(rem, gram_ref, grad_ref, one_ref, two_ref, weight_ref):
    reps = grad_ref.shape[1]
    rows = grad_ref.shape[2]

    @pl.when(pl.program_id(0) == 0)
    def _():
        total = jnp.sum(gram_ref[...], axis=0)
        lane = lax.broadcasted_iota(jnp.int32, (reps, MAIN), 1)
        weights = []
        for layer in range(2):
            parts = [total[:, (2 * layer + h) * 32 : (2 * layer + h + 1) * 32] for h in range(2)]
            weights.append(
                jnp.broadcast_to(tree_weights(jnp.concatenate(parts, axis=0)), (reps, MAIN))
            )
        weight_ref[0] = weights[0]
        weight_ref[1] = weights[1]
        weight_ref[2] = jnp.where(lane < rem, weights[0], weights[1])

    sums = []
    for part in range(3):
        acc = jnp.zeros((rows, MAIN), jnp.float32)
        for r in range(reps):
            acc += weight_ref[part, r : r + 1, :] * grad_ref[part, r].astype(jnp.float32)
        sums.append(acc)
    for layer, ref in enumerate((one_ref, two_ref)):
        ref[:, :MAIN] = sums[layer]
        ref[:, MAIN:] = sums[2][:, layer * rem : (layer + 1) * rem]


def combine(gram_parts, grads, rem):
    _, reps, rows, _ = grads.shape
    block = 64
    cols = MAIN + rem
    return pl.pallas_call(
        functools.partial(combine_kernel, rem),
        grid=(rows // block,),
        in_specs=[
            pl.BlockSpec(gram_parts.shape, lambda i: (0, 0, 0)),
            pl.BlockSpec((3, reps, block, MAIN), lambda i: (0, 0, i, 0)),
        ],
        out_specs=[pl.BlockSpec((block, cols), lambda i: (i, 0))] * 2,
        out_shape=[jax.ShapeDtypeStruct((rows, cols), jnp.float32)] * 2,
        scratch_shapes=[pltpu.VMEM((3, reps, MAIN), jnp.float32)],
        compiler_params=pltpu.CompilerParams(vmem_limit_bytes=32 * 1024 * 1024),
    )(gram_parts, grads)


def core_columns(one, two, core, cols):
    a, b = one[:, core * cols : (core + 1) * cols], two[:, core * cols : (core + 1) * cols]
    return jnp.concatenate([a[:, :MAIN], b[:, :MAIN], a[:, MAIN:], b[:, MAIN:]], axis=1)


def shards(context_one, cotangent_one, context_two, cotangent_two):
    tokens, feats = context_one.shape
    reps = lax.axis_size("replica")
    n_shards = lax.axis_size("shard")
    cols = feats // 2
    core = lax.axis_index("replica") % 2
    same_core = [list(range(c, reps, 2)) for c in range(2)]

    ctx = jnp.concatenate([context_one.T, context_two.T], axis=0)
    ctx = lax.all_gather(ctx, "replica")

    low = core_columns(cotangent_one, cotangent_two, 0, cols)
    high = core_columns(cotangent_one, cotangent_two, 1, cols)
    keep = jnp.where(core == 0, low, high)
    give = jnp.where(core == 0, high, low)
    got = lax.ppermute(give, "replica", [(i, i ^ 1) for i in range(reps)])
    first = jnp.where(core == 0, keep, got)
    second = jnp.where(core == 0, got, keep)
    cot = jnp.concatenate(
        [first[:, : 2 * MAIN], second[:, : 2 * MAIN], first[:, 2 * MAIN :], second[:, 2 * MAIN :]],
        axis=1,
    )
    cot = cot.reshape(n_shards, tokens // n_shards, cot.shape[1])
    cot = lax.all_to_all(cot, "shard", 0, 0)
    cot = lax.all_to_all(cot, "replica", 0, 0, axis_index_groups=same_core)
    pieces_x, pieces_y = gather_pieces(cot)

    offsets = piece_offsets(tokens // n_shards)
    grads, gram = gradients(ctx, pieces_x, pieces_y, offsets, n_shards, tokens)
    gram = jnp.sum(lax.all_to_all(gram, "shard", 0, 0), axis=0)
    gram = lax.all_to_all(jnp.broadcast_to(gram[None], (reps,) + gram.shape), "replica", 0, 0)
    one, two = combine(gram, grads, cols - MAIN)
    return one, two


def solution(mesh):
    spec = P("replica", "shard")
    return jax.shard_map(
        shards,
        mesh=mesh,
        in_specs=(spec, spec, spec, spec),
        out_specs=(P("shard", "replica"), P("shard", "replica")),
        check_vma=False,
    )
```

```python
import functools

import jax
import jax.numpy as jnp
import numpy as np
from jax import lax
from jax.experimental import pallas as pl
from jax.experimental.pallas import tpu as pltpu
from jax.sharding import PartitionSpec as P

EPSILON = 1e-06
SIDE = 4
MAIN = 128
SHIFTS = (0, 1, -1, 2)


def plane_moves(reps, stage, d):
    moves = []
    for r in range(reps):
        for y in range(SIDE):
            for x in range(SIDE):
                if (r + stage) % 2:
                    to = y * SIDE + (x + d) % SIDE
                else:
                    to = ((y + d) % SIDE) * SIDE + x
                moves.append((r * SIDE * SIDE + y * SIDE + x, r * SIDE * SIDE + to))
    return moves


def gather_pieces(piece, reps):
    def move(value, stage, d):
        return lax.ppermute(value, ("replica", "shard"), plane_moves(reps, stage, d))

    after, before, far = [move(piece, 0, d) for d in SHIFTS[1:]]
    low, high = jnp.stack([piece, after]), jnp.stack([before, far])
    low_after = move(low, 1, 1)
    high_before = move(high, 1, -1)
    low_before = move(low, 1, -1)
    high_after = move(high, 1, 1)
    low_far = move(low_after, 1, 1)
    high_far = move(high_before, 1, -1)
    return [low, high, low_after, high_after, low_before, high_before, low_far, high_far]


def piece_offsets(tokens_piece):
    me = lax.axis_index("shard")
    core = lax.axis_index("replica") % 2
    y, x = me // SIDE, me % SIDE
    d = jnp.array(SHIFTS, jnp.int32)
    first, second = d[None, :], d[:, None]
    off_0 = ((y - second) % SIDE) * SIDE + (x - first) % SIDE
    off_1 = ((y - first) % SIDE) * SIDE + (x - second) % SIDE
    off = jnp.where(core == 1, off_0, off_1)
    return (off * tokens_piece).astype(jnp.int32).reshape(-1)


def gradient_kernel(off_ref, ctx_hbm, *refs):
    pieces = refs[:8]
    grad_hbm, gram_ref, ctx_ref, cot_ref, grad_ref, acc_ref, ctx_sems, cot_sems, grad_sems = refs[8:]
    chips, _, _, rows, tokens = ctx_hbm.shape
    _, _, tok, width = pieces[0].shape
    reps = 2 * chips
    rem = (width - 4 * MAIN) // 4
    fold = MAIN // rem
    low = rows // fold
    groups = cot_sems.shape[0]
    span = chips // groups

    def ctx_copy(chip):
        return pltpu.make_async_copy(ctx_hbm.at[chip], ctx_ref.at[chip], ctx_sems.at[chip])

    def cot_copy(group, second, first):
        off = pl.multiple_of(off_ref[second * 4 + first], tok)
        part = pl.ds(group * span, span)
        return pltpu.make_async_copy(
            pieces[second * 2 + first // 2].at[first % 2, part],
            cot_ref.at[part, pl.ds(off, tok), :],
            cot_sems.at[group, second, first],
        )

    def grad_copy(chip):
        part = pl.ds(chip * 2, 2)
        return pltpu.make_async_copy(
            grad_ref.at[:, part], grad_hbm.at[:, part], grad_sems.at[chip]
        )

    for group in range(groups):
        for second in range(4):
            for first in range(4):
                cot_copy(group, second, first).start()
        for chip in range(group * span, (group + 1) * span):
            ctx_copy(chip).start()

    quarter = lax.broadcasted_iota(jnp.int32, (low, MAIN), 1) // rem

    def one_chip(chip, carry):
        ctx_copy(chip).wait()
        edge = cot_ref[chip, :, 4 * MAIN :]
        for core in range(2):
            for layer in range(2):
                j = 2 * core + layer
                rhs = jnp.concatenate([cot_ref[chip, :, j * MAIN : (j + 1) * MAIN], edge], axis=1)
                g = jnp.dot(ctx_ref[chip, core, layer], rhs, preferred_element_type=jnp.float32)
                packed = None
                for q in range(fold):
                    part = g[q * low : (q + 1) * low, MAIN:]
                    if (q - j) % fold:
                        part = pltpu.roll(part, ((q - j) % fold) * rem, 1)
                    packed = part if packed is None else jnp.where(quarter == q, part, packed)
                for at, size, value in ((0, rows, g[:, :MAIN]), (rows, low, packed)):
                    grad_ref[layer, chip * 2 + core, at : at + size] = value.astype(jnp.bfloat16)
        grad_copy(chip).start()
        return carry

    for group in range(groups):
        for second in range(4):
            for first in range(4):
                cot_copy(group, second, first).wait()
        lax.fori_loop(group * span, (group + 1) * span, one_chip, 0)

    size = reps * 8
    deep = 5
    acc_ref[...] = jnp.zeros_like(acc_ref)

    def body(i, carry):
        for layer in range(2):
            parts = []
            for u in range(deep):
                at = pl.multiple_of((i * deep + u) * 16, 16)
                part = grad_ref[layer, :, pl.ds(at, 16), :].astype(jnp.float32)
                part = part.reshape(reps, 2, 8, MAIN)
                for h in range(2):
                    parts.append(part[:, h].reshape(size, MAIN).astype(jnp.bfloat16))
            part = jnp.concatenate(parts, axis=1)
            acc_ref[layer] += lax.dot_general(
                part, part, (((1,), (1,)), ((), ())), preferred_element_type=jnp.float32
            )
        return carry

    lax.fori_loop(0, (rows + low) // (16 * deep), body, 0)
    ri = lax.broadcasted_iota(jnp.int32, (size, size), 0)
    ci = lax.broadcasted_iota(jnp.int32, (size, size), 1)
    si = lax.broadcasted_iota(jnp.int32, (size, MAIN), 0)
    sj = lax.broadcasted_iota(jnp.int32, (size, MAIN), 1)
    rows_of = []
    for layer in range(2):
        z = jnp.where(ri % 8 == ci % 8, acc_ref[layer], 0.0)
        rows_of.append(jnp.sum(z.reshape(reps, 8, size), axis=1))
    pick = jnp.where(sj % 32 == si // 8, 1.0, 0.0)
    z = jnp.dot(
        jnp.concatenate(rows_of, axis=0),
        pick,
        precision=lax.Precision.HIGHEST,
        preferred_element_type=jnp.float32,
    )
    place = lax.broadcasted_iota(jnp.int32, (16, MAIN), 1) // 32
    total = z[:16]
    for k in range(1, 4):
        total = jnp.where(place == k, z[16 * k : 16 * (k + 1)], total)
    gram_ref[...] = total
    for chip in range(chips):
        grad_copy(chip).wait()


def gradients(ctx, pieces, offsets, tokens):
    reps, rows2, _ = ctx.shape
    rows = rows2 // 2
    rem = (pieces[0].shape[-1] - 4 * MAIN) // 4
    _, chips, tok, width = pieces[0].shape
    held = rows + rows * rem // MAIN
    groups = 4
    ctx = ctx.reshape(chips, 2, 2, rows, tokens)
    return pl.pallas_call(
        gradient_kernel,
        in_specs=[pl.BlockSpec(memory_space=pltpu.SMEM)] + [pl.BlockSpec(memory_space=pltpu.HBM)] * 9,
        out_specs=[pl.BlockSpec(memory_space=pltpu.HBM), pl.BlockSpec(memory_space=pltpu.VMEM)],
        scratch_shapes=[
            pltpu.VMEM((chips, 2, 2, rows, tokens), jnp.bfloat16),
            pltpu.VMEM((chips, tokens, width), jnp.bfloat16),
            pltpu.VMEM((2, reps, held, MAIN), jnp.bfloat16),
            pltpu.VMEM((2, reps * 8, reps * 8), jnp.float32),
            pltpu.SemaphoreType.DMA((chips,)),
            pltpu.SemaphoreType.DMA((groups, 4, 4)),
            pltpu.SemaphoreType.DMA((chips,)),
        ],
        out_shape=[
            jax.ShapeDtypeStruct((2, reps, held, MAIN), jnp.bfloat16),
            jax.ShapeDtypeStruct((16, MAIN), jnp.float32),
        ],
        compiler_params=pltpu.CompilerParams(vmem_limit_bytes=48 * 1024 * 1024),
    )(offsets, ctx, *pieces)


def tree_weights(gram):
    n = gram.shape[0]
    ri = lax.broadcasted_iota(jnp.int32, (n, n), 0)
    ci = lax.broadcasted_iota(jnp.int32, (n, n), 1)
    weight = jnp.ones((n, 1), jnp.float32)
    for k in range(n.bit_length() - 1):
        same = (ri >> k) == (ci >> k)
        other = (ri >> k) == ((ci >> k) ^ 1)
        twin = ri == (ci ^ (1 << k))
        own = jnp.where(same, gram, 0.0)
        cross = jnp.where(other, gram, 0.0)
        coeffs = []
        for axis in (1, 0):
            norm = jnp.sum(own, axis=1 - axis, keepdims=True)
            norm = jnp.sum(jnp.where(same, norm, 0.0), axis=axis, keepdims=True)
            inner = jnp.sum(cross, axis=1 - axis, keepdims=True)
            inner = jnp.sum(jnp.where(same, inner, 0.0), axis=axis, keepdims=True)
            coeffs.append((jnp.maximum(norm, 0.0), inner))
        (norm_r, inner_r), (norm_c, inner_c) = coeffs
        twin_r = jnp.sum(jnp.where(twin, norm_c, 0.0), axis=1, keepdims=True)
        twin_c = jnp.sum(jnp.where(twin, norm_r, 0.0), axis=0, keepdims=True)
        cap_r = jnp.sqrt(norm_r) * jnp.sqrt(twin_r)
        cap_c = jnp.sqrt(norm_c) * jnp.sqrt(twin_c)
        inner_r = jnp.clip(inner_r, -cap_r, cap_r)
        inner_c = jnp.clip(inner_c, -cap_c, cap_c)
        coeff_r = 1.0 - inner_r / (2.0 * (norm_r + EPSILON))
        coeff_c = 1.0 - inner_c / (2.0 * (norm_c + EPSILON))
        weight = weight * coeff_r
        gram = gram * coeff_r * coeff_c
    return weight


def combine_kernel(scale, gram_ref, grad_hbm, one_hbm, two_hbm, *scratch):
    grad_ref, one_ref, two_ref, weight_ref, grad_sems, out_sems = scratch
    _, reps, held, _ = grad_ref.shape
    cols, rows = one_ref.shape
    rem = cols - MAIN
    low = held - rows
    starts = range(0, held, low)

    def grad_copy(layer, k):
        part = pl.ds(k * low, low)
        return pltpu.make_async_copy(
            grad_hbm.at[layer, :, part], grad_ref.at[layer, :, part], grad_sems.at[layer, k]
        )

    for layer in range(2):
        for k in range(len(starts)):
            grad_copy(layer, k).start()
    total = jnp.sum(gram_ref[...], axis=0) * (scale * scale)
    for layer in range(2):
        parts = [total[:, (2 * layer + h) * 32 : (2 * layer + h + 1) * 32] for h in range(2)]
        weights = tree_weights(jnp.concatenate(parts, axis=0))
        weight_ref[layer] = jnp.broadcast_to(weights * scale, (reps, MAIN))
    outs = []
    for layer, (out_ref, out_hbm) in enumerate(((one_ref, one_hbm), (two_ref, two_hbm))):
        sums = []
        for k, at in enumerate(starts):
            grad_copy(layer, k).wait()
            acc = jnp.zeros((low, MAIN), jnp.float32)
            for r in range(reps):
                value = grad_ref[layer, r, at : at + low].astype(jnp.float32)
                acc += weight_ref[layer, r : r + 1, :] * value
            sums.append(acc)
        out_ref[:MAIN] = jnp.concatenate(sums[:-1], axis=0).T
        edge = sums[-1].T
        for q in range(MAIN // rem):
            out_ref[MAIN:, q * low : (q + 1) * low] = edge[q * rem : (q + 1) * rem]
        outs.append(pltpu.make_async_copy(out_ref, out_hbm, out_sems.at[layer]))
        outs[-1].start()
    for out in outs:
        out.wait()


def combine(gram_parts, grads, rows, cols, scale):
    out = pltpu.HBM((cols, rows), jnp.float32)
    grads = pltpu.with_memory_space_constraint(grads, pltpu.HBM)
    held = grads.shape[2]
    return pl.pallas_call(
        functools.partial(combine_kernel, scale),
        in_specs=[pl.BlockSpec(memory_space=pltpu.VMEM), pl.BlockSpec(memory_space=pltpu.HBM)],
        out_specs=[pl.BlockSpec(memory_space=pltpu.HBM)] * 2,
        out_shape=[out] * 2,
        scratch_shapes=[
            pltpu.VMEM(grads.shape, grads.dtype),
            pltpu.VMEM((cols, rows), jnp.float32),
            pltpu.VMEM((cols, rows), jnp.float32),
            pltpu.VMEM((2, grads.shape[1], MAIN), jnp.float32),
            pltpu.SemaphoreType.DMA((2, held // (held - rows))),
            pltpu.SemaphoreType.DMA((2,)),
        ],
        compiler_params=pltpu.CompilerParams(vmem_limit_bytes=32 * 1024 * 1024),
    )(gram_parts, grads)


def split_kernel(core_ref, a_ref, b_ref, one_ref, two_ref, ctx_ref, keep_ref, give_ref):
    rows = a_ref.shape[0]
    cols = rows // 2
    rem = cols - MAIN
    ctx_ref[:rows] = a_ref[...]
    ctx_ref[rows:] = b_ref[...]

    def fill(out_ref, core):
        for layer, ref in enumerate((one_ref, two_ref)):
            at = core * cols
            out_ref[layer * MAIN : (layer + 1) * MAIN] = ref[at : at + MAIN]
            to = 2 * MAIN + layer * rem
            out_ref[to : to + rem] = ref[at + MAIN : at + cols]

    for core in range(2):

        @pl.when(core_ref[0] == core)
        def _():
            fill(give_ref, 1 - core)
            fill(keep_ref, core)


def split_columns(core, contexts, cotangents):
    shape, dtype = contexts[0].shape, contexts[0].dtype
    return pl.pallas_call(
        split_kernel,
        in_specs=[pl.BlockSpec(memory_space=pltpu.SMEM)]
        + [pl.BlockSpec(memory_space=pltpu.VMEM)] * 4,
        out_specs=[pl.BlockSpec(memory_space=pltpu.VMEM)] * 3,
        out_shape=[
            jax.ShapeDtypeStruct((2 * shape[0], shape[1]), dtype),
            jax.ShapeDtypeStruct(shape, dtype),
            jax.ShapeDtypeStruct(shape, dtype),
        ],
    )(core, *contexts, *cotangents)


def join_kernel(core_ref, keep_ref, got_ref, out_ref):
    main = 2 * MAIN

    def fill(first, second):
        parts = [first[:main], second[:main], first[main:], second[main:]]
        out_ref[...] = jnp.concatenate(parts, axis=0).T

    for core, (first, second) in enumerate(((keep_ref, got_ref), (got_ref, keep_ref))):

        @pl.when(core_ref[0] == core)
        def _():
            fill(first, second)


def join_columns(core, keep, got):
    cols, tokens = keep.shape
    return pl.pallas_call(
        join_kernel,
        in_specs=[pl.BlockSpec(memory_space=pltpu.SMEM)]
        + [pl.BlockSpec(memory_space=pltpu.VMEM)] * 2,
        out_specs=pl.BlockSpec(memory_space=pltpu.VMEM),
        out_shape=jax.ShapeDtypeStruct((tokens, 2 * cols), keep.dtype),
    )(core, keep, got)


def shards(context_one, cotangent_one, context_two, cotangent_two):
    tokens, feats = context_one.shape
    reps = lax.axis_size("replica")
    n_shards = lax.axis_size("shard")
    cols = feats // 2
    core = (lax.axis_index("replica") % 2).reshape(1).astype(jnp.int32)
    same_core = [list(range(c, reps, 2)) for c in range(2)]

    ctx, keep, give = split_columns(
        core, (context_one.T, context_two.T), (cotangent_one.T, cotangent_two.T)
    )
    ctx = lax.all_gather(ctx, "replica")
    got = lax.ppermute(give, "replica", [(i, i ^ 1) for i in range(reps)])
    cot = join_columns(core, keep, got)
    cot = cot.reshape(n_shards, tokens // n_shards, cot.shape[1])
    cot = lax.all_to_all(cot, "shard", 0, 0)
    cot = lax.all_to_all(cot, "replica", 0, 0, axis_index_groups=same_core)
    pieces = gather_pieces(cot, reps)

    offsets = piece_offsets(tokens // n_shards)
    grads, gram = gradients(ctx, pieces, offsets, tokens)
    gram = gram + lax.ppermute(gram, "replica", [(i, i ^ 1) for i in range(reps)])
    gram = jnp.broadcast_to(gram[None], (n_shards,) + gram.shape)
    gram = jnp.sum(lax.all_to_all(gram, "shard", 0, 0), axis=0)
    gram = jnp.broadcast_to(gram[None], (reps // 2,) + gram.shape)
    gram = lax.all_to_all(gram, "replica", 0, 0, axis_index_groups=same_core)
    one, two = combine(gram, grads, feats, cols, 1.0 / tokens)
    return one.T, two.T


def solution(mesh):
    spec = P("replica", "shard")
    return jax.shard_map(
        shards,
        mesh=mesh,
        in_specs=(spec, spec, spec, spec),
        out_specs=(P("shard", "replica"), P("shard", "replica")),
        check_vma=False,
    )
```

```python
import functools

import jax
import jax.numpy as jnp
import numpy as np
from jax import lax
from jax.experimental import pallas as pl
from jax.experimental.pallas import tpu as pltpu
from jax.sharding import PartitionSpec as P

EPSILON = 1e-06
SIDE = 4
MAIN = 128
SHIFTS = (0, 1, -1, 2)


def plane_moves(reps, stage, d):
    moves = []
    for r in range(reps):
        for y in range(SIDE):
            for x in range(SIDE):
                if (r + stage) % 2:
                    to = y * SIDE + (x + d) % SIDE
                else:
                    to = ((y + d) % SIDE) * SIDE + x
                moves.append((r * SIDE * SIDE + y * SIDE + x, r * SIDE * SIDE + to))
    return moves


def gather_pieces(piece, reps):
    def move(value, stage, d):
        return lax.ppermute(value, ("replica", "shard"), plane_moves(reps, stage, d))

    after, before, far = [move(piece, 0, d) for d in SHIFTS[1:]]
    low, high = jnp.stack([piece, after]), jnp.stack([before, far])
    low_after = move(low, 1, 1)
    high_before = move(high, 1, -1)
    low_before = move(low, 1, -1)
    high_after = move(high, 1, 1)
    low_far = move(low_after, 1, 1)
    high_far = move(high_before, 1, -1)
    return [low, high, low_after, high_after, low_before, high_before, low_far, high_far]


def piece_offsets(tokens_piece):
    me = lax.axis_index("shard")
    core = lax.axis_index("replica") % 2
    y, x = me // SIDE, me % SIDE
    d = jnp.array(SHIFTS, jnp.int32)
    first, second = d[None, :], d[:, None]
    off_0 = ((y - second) % SIDE) * SIDE + (x - first) % SIDE
    off_1 = ((y - first) % SIDE) * SIDE + (x - second) % SIDE
    off = jnp.where(core == 1, off_0, off_1)
    return (off * tokens_piece).astype(jnp.int32).reshape(-1)


def gradient_kernel(off_ref, ctx_hbm, *refs):
    pieces = refs[:8]
    grad_hbm, gram_ref, ctx_ref, cot_ref, grad_ref, acc_ref, ctx_sems, cot_sems, grad_sems = refs[8:]
    chips, _, _, rows, tokens = ctx_hbm.shape
    _, _, tok, width = pieces[0].shape
    reps = 2 * chips
    rem = (width - 4 * MAIN) // 4
    fold = MAIN // rem
    low = rows // fold
    groups = cot_sems.shape[0]
    span = chips // groups

    def ctx_copy(chip):
        return pltpu.make_async_copy(ctx_hbm.at[chip], ctx_ref.at[chip], ctx_sems.at[chip])

    def cot_copy(group, second, first):
        off = pl.multiple_of(off_ref[second * 4 + first], tok)
        part = pl.ds(group * span, span)
        return pltpu.make_async_copy(
            pieces[second * 2 + first // 2].at[first % 2, part],
            cot_ref.at[part, pl.ds(off, tok), :],
            cot_sems.at[group, second, first],
        )

    def grad_copy(chip):
        part = pl.ds(chip * 2, 2)
        return pltpu.make_async_copy(
            grad_ref.at[:, part], grad_hbm.at[:, part], grad_sems.at[chip]
        )

    for group in range(groups):
        for second in range(4):
            for first in range(4):
                cot_copy(group, second, first).start()
        for chip in range(group * span, (group + 1) * span):
            ctx_copy(chip).start()

    quarter = lax.broadcasted_iota(jnp.int32, (low, MAIN), 1) // rem

    def one_chip(chip, carry):
        ctx_copy(chip).wait()
        edge = cot_ref[chip, :, 4 * MAIN :]
        for core in range(2):
            for layer in range(2):
                j = 2 * core + layer
                rhs = jnp.concatenate([cot_ref[chip, :, j * MAIN : (j + 1) * MAIN], edge], axis=1)
                g = jnp.dot(ctx_ref[chip, core, layer], rhs, preferred_element_type=jnp.float32)
                packed = None
                for q in range(fold):
                    part = g[q * low : (q + 1) * low, MAIN:]
                    if (q - j) % fold:
                        part = pltpu.roll(part, ((q - j) % fold) * rem, 1)
                    packed = part if packed is None else jnp.where(quarter == q, part, packed)
                for at, size, value in ((0, rows, g[:, :MAIN]), (rows, low, packed)):
                    grad_ref[layer, chip * 2 + core, at : at + size] = value.astype(jnp.bfloat16)
        grad_copy(chip).start()
        return carry

    for group in range(groups):
        for second in range(4):
            for first in range(4):
                cot_copy(group, second, first).wait()
        lax.fori_loop(group * span, (group + 1) * span, one_chip, 0)

    size = reps * 8
    deep = 5
    acc_ref[...] = jnp.zeros_like(acc_ref)

    def body(i, carry):
        for layer in range(2):
            parts = []
            for u in range(deep):
                at = pl.multiple_of((i * deep + u) * 16, 16)
                part = grad_ref[layer, :, pl.ds(at, 16), :].astype(jnp.float32)
                part = part.reshape(reps, 2, 8, MAIN)
                for h in range(2):
                    parts.append(part[:, h].reshape(size, MAIN).astype(jnp.bfloat16))
            part = jnp.concatenate(parts, axis=1)
            acc_ref[layer] += lax.dot_general(
                part, part, (((1,), (1,)), ((), ())), preferred_element_type=jnp.float32
            )
        return carry

    lax.fori_loop(0, (rows + low) // (16 * deep), body, 0)
    ri = lax.broadcasted_iota(jnp.int32, (size, size), 0)
    ci = lax.broadcasted_iota(jnp.int32, (size, size), 1)
    si = lax.broadcasted_iota(jnp.int32, (size, MAIN), 0)
    sj = lax.broadcasted_iota(jnp.int32, (size, MAIN), 1)
    rows_of = []
    for layer in range(2):
        z = jnp.where(ri % 8 == ci % 8, acc_ref[layer], 0.0)
        rows_of.append(jnp.sum(z.reshape(reps, 8, size), axis=1))
    pick = jnp.where(sj % 32 == si // 8, 1.0, 0.0)
    z = jnp.dot(
        jnp.concatenate(rows_of, axis=0),
        pick,
        precision=lax.Precision.HIGHEST,
        preferred_element_type=jnp.float32,
    )
    place = lax.broadcasted_iota(jnp.int32, (16, MAIN), 1) // 32
    total = z[:16]
    for k in range(1, 4):
        total = jnp.where(place == k, z[16 * k : 16 * (k + 1)], total)
    gram_ref[...] = total
    for chip in range(chips):
        grad_copy(chip).wait()


def gradients(ctx, pieces, offsets, tokens):
    reps, rows2, _ = ctx.shape
    rows = rows2 // 2
    rem = (pieces[0].shape[-1] - 4 * MAIN) // 4
    _, chips, tok, width = pieces[0].shape
    held = rows + rows * rem // MAIN
    groups = 1
    ctx = ctx.reshape(chips, 2, 2, rows, tokens)
    return pl.pallas_call(
        gradient_kernel,
        in_specs=[pl.BlockSpec(memory_space=pltpu.SMEM)] + [pl.BlockSpec(memory_space=pltpu.HBM)] * 9,
        out_specs=[pl.BlockSpec(memory_space=pltpu.HBM), pl.BlockSpec(memory_space=pltpu.VMEM)],
        scratch_shapes=[
            pltpu.VMEM((chips, 2, 2, rows, tokens), jnp.bfloat16),
            pltpu.VMEM((chips, tokens, width), jnp.bfloat16),
            pltpu.VMEM((2, reps, held, MAIN), jnp.bfloat16),
            pltpu.VMEM((2, reps * 8, reps * 8), jnp.float32),
            pltpu.SemaphoreType.DMA((chips,)),
            pltpu.SemaphoreType.DMA((groups, 4, 4)),
            pltpu.SemaphoreType.DMA((chips,)),
        ],
        out_shape=[
            jax.ShapeDtypeStruct((2, reps, held, MAIN), jnp.bfloat16),
            jax.ShapeDtypeStruct((16, MAIN), jnp.float32),
        ],
        compiler_params=pltpu.CompilerParams(vmem_limit_bytes=48 * 1024 * 1024),
    )(offsets, ctx, *pieces)


def tree_weights(gram):
    n = gram.shape[0]
    ri = lax.broadcasted_iota(jnp.int32, (n, n), 0)
    ci = lax.broadcasted_iota(jnp.int32, (n, n), 1)
    weight = jnp.ones((n, 1), jnp.float32)
    for k in range(n.bit_length() - 1):
        same = (ri >> k) == (ci >> k)
        other = (ri >> k) == ((ci >> k) ^ 1)
        twin = ri == (ci ^ (1 << k))
        own = jnp.where(same, gram, 0.0)
        cross = jnp.where(other, gram, 0.0)
        coeffs = []
        for axis in (1, 0):
            norm = jnp.sum(own, axis=1 - axis, keepdims=True)
            norm = jnp.sum(jnp.where(same, norm, 0.0), axis=axis, keepdims=True)
            inner = jnp.sum(cross, axis=1 - axis, keepdims=True)
            inner = jnp.sum(jnp.where(same, inner, 0.0), axis=axis, keepdims=True)
            coeffs.append((jnp.maximum(norm, 0.0), inner))
        (norm_r, inner_r), (norm_c, inner_c) = coeffs
        twin_r = jnp.sum(jnp.where(twin, norm_c, 0.0), axis=1, keepdims=True)
        twin_c = jnp.sum(jnp.where(twin, norm_r, 0.0), axis=0, keepdims=True)
        cap_r = jnp.sqrt(norm_r) * jnp.sqrt(twin_r)
        cap_c = jnp.sqrt(norm_c) * jnp.sqrt(twin_c)
        inner_r = jnp.clip(inner_r, -cap_r, cap_r)
        inner_c = jnp.clip(inner_c, -cap_c, cap_c)
        coeff_r = 1.0 - inner_r / (2.0 * (norm_r + EPSILON))
        coeff_c = 1.0 - inner_c / (2.0 * (norm_c + EPSILON))
        weight = weight * coeff_r
        gram = gram * coeff_r * coeff_c
    return weight


def combine_kernel(scale, gram_ref, grad_hbm, one_hbm, two_hbm, *scratch):
    grad_ref, one_ref, two_ref, weight_ref, grad_sems, out_sems = scratch
    _, reps, held, _ = grad_ref.shape
    cols, rows = one_ref.shape
    rem = cols - MAIN
    low = held - rows
    starts = range(0, held, low)

    def grad_copy(layer, k):
        part = pl.ds(k * low, low)
        return pltpu.make_async_copy(
            grad_hbm.at[layer, :, part], grad_ref.at[layer, :, part], grad_sems.at[layer, k]
        )

    for layer in range(2):
        for k in range(len(starts)):
            grad_copy(layer, k).start()
    total = jnp.sum(gram_ref[...], axis=0) * (scale * scale)
    for layer in range(2):
        parts = [total[:, (2 * layer + h) * 32 : (2 * layer + h + 1) * 32] for h in range(2)]
        weights = tree_weights(jnp.concatenate(parts, axis=0))
        weight_ref[layer] = jnp.broadcast_to(weights * scale, (reps, MAIN))
    outs = []
    for layer, (out_ref, out_hbm) in enumerate(((one_ref, one_hbm), (two_ref, two_hbm))):
        sums = []
        for k, at in enumerate(starts):
            grad_copy(layer, k).wait()
            acc = jnp.zeros((low, MAIN), jnp.float32)
            for r in range(reps):
                value = grad_ref[layer, r, at : at + low].astype(jnp.float32)
                acc += weight_ref[layer, r : r + 1, :] * value
            sums.append(acc)
        out_ref[:MAIN] = jnp.concatenate(sums[:-1], axis=0).T
        edge = sums[-1].T
        for q in range(MAIN // rem):
            out_ref[MAIN:, q * low : (q + 1) * low] = edge[q * rem : (q + 1) * rem]
        outs.append(pltpu.make_async_copy(out_ref, out_hbm, out_sems.at[layer]))
        outs[-1].start()
    for out in outs:
        out.wait()


def combine(gram_parts, grads, rows, cols, scale):
    out = pltpu.HBM((cols, rows), jnp.float32)
    grads = pltpu.with_memory_space_constraint(grads, pltpu.HBM)
    held = grads.shape[2]
    return pl.pallas_call(
        functools.partial(combine_kernel, scale),
        in_specs=[pl.BlockSpec(memory_space=pltpu.VMEM), pl.BlockSpec(memory_space=pltpu.HBM)],
        out_specs=[pl.BlockSpec(memory_space=pltpu.HBM)] * 2,
        out_shape=[out] * 2,
        scratch_shapes=[
            pltpu.VMEM(grads.shape, grads.dtype),
            pltpu.VMEM((cols, rows), jnp.float32),
            pltpu.VMEM((cols, rows), jnp.float32),
            pltpu.VMEM((2, grads.shape[1], MAIN), jnp.float32),
            pltpu.SemaphoreType.DMA((2, held // (held - rows))),
            pltpu.SemaphoreType.DMA((2,)),
        ],
        compiler_params=pltpu.CompilerParams(vmem_limit_bytes=32 * 1024 * 1024),
    )(gram_parts, grads)


def stack_kernel(one_ref, two_ref, out_ref):
    rows = one_ref.shape[0]
    out_ref[:rows] = one_ref[...]
    out_ref[rows:] = two_ref[...]


def stack_contexts(one, two):
    rows, tokens = one.shape
    return pl.pallas_call(
        stack_kernel,
        in_specs=[pl.BlockSpec(memory_space=pltpu.VMEM)] * 2,
        out_specs=pl.BlockSpec(memory_space=pltpu.VMEM),
        out_shape=jax.ShapeDtypeStruct((2 * rows, tokens), one.dtype),
    )(one, two)


def split_kernel(one_ref, two_ref, out_ref):
    cols = one_ref.shape[0] // 2
    shards = out_ref.shape[0] // 2
    both = (one_ref, two_ref)
    for core in range(2):
        at = core * cols
        parts = [ref[at : at + MAIN] for ref in both] + [ref[at + MAIN : at + cols] for ref in both]
        value = jnp.concatenate(parts, axis=0).T
        out_ref[core * shards : (core + 1) * shards] = value.reshape((shards,) + out_ref.shape[1:])


def split_cotangents(one, two, shards):
    cols, tokens = one.shape
    return pl.pallas_call(
        split_kernel,
        in_specs=[pl.BlockSpec(memory_space=pltpu.VMEM)] * 2,
        out_specs=pl.BlockSpec(memory_space=pltpu.VMEM),
        out_shape=jax.ShapeDtypeStruct((2 * shards, tokens // shards, cols), one.dtype),
    )(one, two)


def join_kernel(got_ref, out_ref):
    shards, tok, width = out_ref.shape
    main = 2 * MAIN
    sides = [
        got_ref[c * shards : (c + 1) * shards].reshape(shards * tok, width // 2) for c in range(2)
    ]
    for c in range(2):
        out_ref[:, :, c * main : (c + 1) * main] = sides[c][:, :main].reshape(shards, tok, main)
    edges = jnp.concatenate([side[:, main:] for side in sides], axis=1)
    out_ref[:, :, 2 * main :] = edges.reshape(shards, tok, width - 2 * main)


def join_cores(got):
    both, tok, cols = got.shape
    return pl.pallas_call(
        join_kernel,
        in_specs=[pl.BlockSpec(memory_space=pltpu.VMEM)],
        out_specs=pl.BlockSpec(memory_space=pltpu.VMEM),
        out_shape=jax.ShapeDtypeStruct((both // 2, tok, 2 * cols), got.dtype),
    )(got)


def shards(context_one, cotangent_one, context_two, cotangent_two):
    tokens, feats = context_one.shape
    reps = lax.axis_size("replica")
    n_shards = lax.axis_size("shard")
    cols = feats // 2
    same_core = [list(range(c, reps, 2)) for c in range(2)]
    axes = ("replica", "shard")
    size = 2 * n_shards
    planes = [list(range(z * size, (z + 1) * size)) for z in range(reps // 2)]

    ctx = stack_contexts(context_one.T, context_two.T)
    ctx = lax.all_gather(ctx, "replica")
    cot = split_cotangents(cotangent_one.T, cotangent_two.T, n_shards)
    cot = join_cores(lax.all_to_all(cot, axes, 0, 0, axis_index_groups=planes))
    cot = lax.all_to_all(cot, "replica", 0, 0, axis_index_groups=same_core)
    pieces = gather_pieces(cot, reps)

    offsets = piece_offsets(tokens // n_shards)
    grads, gram = gradients(ctx, pieces, offsets, tokens)
    gram = jnp.broadcast_to(gram[None], (size,) + gram.shape)
    gram = jnp.sum(lax.all_to_all(gram, axes, 0, 0, axis_index_groups=planes), axis=0)
    gram = jnp.broadcast_to(gram[None], (reps // 2,) + gram.shape)
    gram = lax.all_to_all(gram, "replica", 0, 0, axis_index_groups=same_core)
    one, two = combine(gram, grads, feats, cols, 1.0 / tokens)
    return one.T, two.T


def solution(mesh):
    spec = P("replica", "shard")
    return jax.shard_map(
        shards,
        mesh=mesh,
        in_specs=(spec, spec, spec, spec),
        out_specs=(P("shard", "replica"), P("shard", "replica")),
        check_vma=False,
    )
```

```python
import functools

import jax
import jax.numpy as jnp
import numpy as np
from jax import lax
from jax.experimental import pallas as pl
from jax.experimental.pallas import tpu as pltpu
from jax.sharding import PartitionSpec as P

EPSILON = 1e-06
SIDE = 4
MAIN = 128
SHIFTS = (0, 1, -1, 2)


def plane_moves(reps, stage, d):
    moves = []
    for r in range(reps):
        for y in range(SIDE):
            for x in range(SIDE):
                if (r + stage) % 2:
                    to = y * SIDE + (x + d) % SIDE
                else:
                    to = ((y + d) % SIDE) * SIDE + x
                moves.append((r * SIDE * SIDE + y * SIDE + x, r * SIDE * SIDE + to))
    return moves


def gather_pieces(piece, reps):
    def move(value, stage, d):
        return lax.ppermute(value, ("replica", "shard"), plane_moves(reps, stage, d))

    after, before, far = [move(piece, 0, d) for d in SHIFTS[1:]]
    low, high = jnp.stack([piece, after]), jnp.stack([before, far])
    low_after = move(low, 1, 1)
    high_before = move(high, 1, -1)
    low_before = move(low, 1, -1)
    high_after = move(high, 1, 1)
    low_far = move(low_after, 1, 1)
    high_far = move(high_before, 1, -1)
    return [low, high, low_after, high_after, low_before, high_before, low_far, high_far]


def piece_offsets(tokens_piece):
    me = lax.axis_index("shard")
    core = lax.axis_index("replica") % 2
    y, x = me // SIDE, me % SIDE
    d = jnp.array(SHIFTS, jnp.int32)
    first, second = d[None, :], d[:, None]
    off_0 = ((y - second) % SIDE) * SIDE + (x - first) % SIDE
    off_1 = ((y - first) % SIDE) * SIDE + (x - second) % SIDE
    off = jnp.where(core == 1, off_0, off_1)
    return (off * tokens_piece).astype(jnp.int32).reshape(-1)


def gradient_kernel(off_ref, ctx_hbm, *refs):
    pieces = refs[:8]
    grad_hbm, gram_ref, ctx_ref, cot_ref, grad_ref, acc_ref, ctx_sems, cot_sems, grad_sems = refs[8:]
    chips, _, _, rows, tokens = ctx_hbm.shape
    _, _, tok, width = pieces[0].shape
    reps = 2 * chips
    rem = (width - 4 * MAIN) // 4
    fold = MAIN // rem
    low = rows // fold
    groups = cot_sems.shape[0]
    span = chips // groups

    def ctx_copy(chip):
        return pltpu.make_async_copy(ctx_hbm.at[chip], ctx_ref.at[chip], ctx_sems.at[chip])

    def cot_copy(group, second, first):
        off = pl.multiple_of(off_ref[second * 4 + first], tok)
        part = pl.ds(group * span, span)
        return pltpu.make_async_copy(
            pieces[second * 2 + first // 2].at[first % 2, part],
            cot_ref.at[part, pl.ds(off, tok), :],
            cot_sems.at[group, second, first],
        )

    def grad_copy(chip):
        part = pl.ds(chip * 2, 2)
        return pltpu.make_async_copy(
            grad_ref.at[:, part], grad_hbm.at[:, part], grad_sems.at[chip]
        )

    for group in range(groups):
        for second in range(4):
            for first in range(4):
                cot_copy(group, second, first).start()
        for chip in range(group * span, (group + 1) * span):
            ctx_copy(chip).start()

    quarter = lax.broadcasted_iota(jnp.int32, (low, MAIN), 1) // rem

    def one_chip(chip, carry):
        ctx_copy(chip).wait()
        edge = cot_ref[chip, :, 4 * MAIN :]
        for core in range(2):
            for layer in range(2):
                j = 2 * core + layer
                rhs = jnp.concatenate([cot_ref[chip, :, j * MAIN : (j + 1) * MAIN], edge], axis=1)
                g = jnp.dot(ctx_ref[chip, core, layer], rhs, preferred_element_type=jnp.float32)
                packed = None
                for q in range(fold):
                    part = g[q * low : (q + 1) * low, MAIN:]
                    if (q - j) % fold:
                        part = pltpu.roll(part, ((q - j) % fold) * rem, 1)
                    packed = part if packed is None else jnp.where(quarter == q, part, packed)
                for at, size, value in ((0, rows, g[:, :MAIN]), (rows, low, packed)):
                    grad_ref[layer, chip * 2 + core, at : at + size] = value.astype(jnp.bfloat16)
        grad_copy(chip).start()
        return carry

    for group in range(groups):
        for second in range(4):
            for first in range(4):
                cot_copy(group, second, first).wait()
        lax.fori_loop(group * span, (group + 1) * span, one_chip, 0)

    size = reps * 8
    deep = 5
    acc_ref[...] = jnp.zeros_like(acc_ref)

    def body(i, carry):
        for layer in range(2):
            parts = []
            for u in range(deep):
                at = pl.multiple_of((i * deep + u) * 16, 16)
                part = grad_ref[layer, :, pl.ds(at, 16), :].astype(jnp.float32)
                part = part.reshape(reps, 2, 8, MAIN)
                for h in range(2):
                    parts.append(part[:, h].reshape(size, MAIN).astype(jnp.bfloat16))
            part = jnp.concatenate(parts, axis=1)
            acc_ref[layer] += lax.dot_general(
                part, part, (((1,), (1,)), ((), ())), preferred_element_type=jnp.float32
            )
        return carry

    lax.fori_loop(0, (rows + low) // (16 * deep), body, 0)
    ri = lax.broadcasted_iota(jnp.int32, (size, size), 0)
    ci = lax.broadcasted_iota(jnp.int32, (size, size), 1)
    si = lax.broadcasted_iota(jnp.int32, (size, MAIN), 0)
    sj = lax.broadcasted_iota(jnp.int32, (size, MAIN), 1)
    rows_of = []
    for layer in range(2):
        z = jnp.where(ri % 8 == ci % 8, acc_ref[layer], 0.0)
        rows_of.append(jnp.sum(z.reshape(reps, 8, size), axis=1))
    pick = jnp.where(sj % 32 == si // 8, 1.0, 0.0)
    z = jnp.dot(
        jnp.concatenate(rows_of, axis=0),
        pick,
        precision=lax.Precision.HIGHEST,
        preferred_element_type=jnp.float32,
    )
    place = lax.broadcasted_iota(jnp.int32, (16, MAIN), 1) // 32
    total = z[:16]
    for k in range(1, 4):
        total = jnp.where(place == k, z[16 * k : 16 * (k + 1)], total)
    gram_ref[...] = total
    for chip in range(chips):
        grad_copy(chip).wait()


def gradients(ctx, pieces, offsets, tokens):
    reps, rows2, _ = ctx.shape
    rows = rows2 // 2
    rem = (pieces[0].shape[-1] - 4 * MAIN) // 4
    _, chips, tok, width = pieces[0].shape
    held = rows + rows * rem // MAIN
    groups = 4
    ctx = ctx.reshape(chips, 2, 2, rows, tokens)
    return pl.pallas_call(
        gradient_kernel,
        in_specs=[pl.BlockSpec(memory_space=pltpu.SMEM)] + [pl.BlockSpec(memory_space=pltpu.HBM)] * 9,
        out_specs=[pl.BlockSpec(memory_space=pltpu.HBM), pl.BlockSpec(memory_space=pltpu.VMEM)],
        scratch_shapes=[
            pltpu.VMEM((chips, 2, 2, rows, tokens), jnp.bfloat16),
            pltpu.VMEM((chips, tokens, width), jnp.bfloat16),
            pltpu.VMEM((2, reps, held, MAIN), jnp.bfloat16),
            pltpu.VMEM((2, reps * 8, reps * 8), jnp.float32),
            pltpu.SemaphoreType.DMA((chips,)),
            pltpu.SemaphoreType.DMA((groups, 4, 4)),
            pltpu.SemaphoreType.DMA((chips,)),
        ],
        out_shape=[
            jax.ShapeDtypeStruct((2, reps, held, MAIN), jnp.bfloat16),
            jax.ShapeDtypeStruct((16, MAIN), jnp.float32),
        ],
        compiler_params=pltpu.CompilerParams(vmem_limit_bytes=48 * 1024 * 1024),
    )(offsets, ctx, *pieces)


def tree_weights(gram):
    n = gram.shape[0]
    ri = lax.broadcasted_iota(jnp.int32, (n, n), 0)
    ci = lax.broadcasted_iota(jnp.int32, (n, n), 1)
    weight = jnp.ones((n, 1), jnp.float32)
    for k in range(n.bit_length() - 1):
        same = (ri >> k) == (ci >> k)
        other = (ri >> k) == ((ci >> k) ^ 1)
        twin = ri == (ci ^ (1 << k))
        own = jnp.where(same, gram, 0.0)
        cross = jnp.where(other, gram, 0.0)
        coeffs = []
        for axis in (1, 0):
            norm = jnp.sum(own, axis=1 - axis, keepdims=True)
            norm = jnp.sum(jnp.where(same, norm, 0.0), axis=axis, keepdims=True)
            inner = jnp.sum(cross, axis=1 - axis, keepdims=True)
            inner = jnp.sum(jnp.where(same, inner, 0.0), axis=axis, keepdims=True)
            coeffs.append((jnp.maximum(norm, 0.0), inner))
        (norm_r, inner_r), (norm_c, inner_c) = coeffs
        twin_r = jnp.sum(jnp.where(twin, norm_c, 0.0), axis=1, keepdims=True)
        twin_c = jnp.sum(jnp.where(twin, norm_r, 0.0), axis=0, keepdims=True)
        cap_r = jnp.sqrt(norm_r) * jnp.sqrt(twin_r)
        cap_c = jnp.sqrt(norm_c) * jnp.sqrt(twin_c)
        inner_r = jnp.clip(inner_r, -cap_r, cap_r)
        inner_c = jnp.clip(inner_c, -cap_c, cap_c)
        coeff_r = 1.0 - inner_r / (2.0 * (norm_r + EPSILON))
        coeff_c = 1.0 - inner_c / (2.0 * (norm_c + EPSILON))
        weight = weight * coeff_r
        gram = gram * coeff_r * coeff_c
    return weight


def combine_kernel(scale, gram_ref, grad_hbm, one_hbm, two_hbm, *scratch):
    grad_ref, one_ref, two_ref, weight_ref, grad_sems, out_sems = scratch
    _, reps, held, _ = grad_ref.shape
    cols, rows = one_ref.shape
    rem = cols - MAIN
    low = held - rows
    starts = range(0, held, low)

    def grad_copy(layer, k):
        part = pl.ds(k * low, low)
        return pltpu.make_async_copy(
            grad_hbm.at[layer, :, part], grad_ref.at[layer, :, part], grad_sems.at[layer, k]
        )

    for layer in range(2):
        for k in range(len(starts)):
            grad_copy(layer, k).start()
    total = jnp.sum(gram_ref[...], axis=0) * (scale * scale)
    for layer in range(2):
        parts = [total[:, (2 * layer + h) * 32 : (2 * layer + h + 1) * 32] for h in range(2)]
        weights = tree_weights(jnp.concatenate(parts, axis=0))
        weight_ref[layer] = jnp.broadcast_to(weights * scale, (reps, MAIN))
    outs = []
    for layer, (out_ref, out_hbm) in enumerate(((one_ref, one_hbm), (two_ref, two_hbm))):
        sums = []
        for k, at in enumerate(starts):
            grad_copy(layer, k).wait()
            acc = jnp.zeros((low, MAIN), jnp.float32)
            for r in range(reps):
                value = grad_ref[layer, r, at : at + low].astype(jnp.float32)
                acc += weight_ref[layer, r : r + 1, :] * value
            sums.append(acc)
        out_ref[:MAIN] = jnp.concatenate(sums[:-1], axis=0).T
        edge = sums[-1].T
        for q in range(MAIN // rem):
            out_ref[MAIN:, q * low : (q + 1) * low] = edge[q * rem : (q + 1) * rem]
        outs.append(pltpu.make_async_copy(out_ref, out_hbm, out_sems.at[layer]))
        outs[-1].start()
    for out in outs:
        out.wait()


def combine(gram_parts, grads, rows, cols, scale):
    out = pltpu.HBM((cols, rows), jnp.float32)
    grads = pltpu.with_memory_space_constraint(grads, pltpu.HBM)
    held = grads.shape[2]
    return pl.pallas_call(
        functools.partial(combine_kernel, scale),
        in_specs=[pl.BlockSpec(memory_space=pltpu.VMEM), pl.BlockSpec(memory_space=pltpu.HBM)],
        out_specs=[pl.BlockSpec(memory_space=pltpu.HBM)] * 2,
        out_shape=[out] * 2,
        scratch_shapes=[
            pltpu.VMEM(grads.shape, grads.dtype),
            pltpu.VMEM((cols, rows), jnp.float32),
            pltpu.VMEM((cols, rows), jnp.float32),
            pltpu.VMEM((2, grads.shape[1], MAIN), jnp.float32),
            pltpu.SemaphoreType.DMA((2, held // (held - rows))),
            pltpu.SemaphoreType.DMA((2,)),
        ],
        compiler_params=pltpu.CompilerParams(vmem_limit_bytes=32 * 1024 * 1024),
    )(gram_parts, grads)


def split_kernel(a_ref, b_ref, one_ref, two_ref, ctx_ref, out_ref):
    rows = a_ref.shape[0]
    cols = rows // 2
    shards = out_ref.shape[0] // 2
    ctx_ref[:rows] = a_ref[...]
    ctx_ref[rows:] = b_ref[...]
    both = (one_ref, two_ref)
    for core in range(2):
        at = core * cols
        parts = [ref[at : at + MAIN] for ref in both] + [ref[at + MAIN : at + cols] for ref in both]
        value = jnp.concatenate(parts, axis=0).T
        out_ref[core * shards : (core + 1) * shards] = value.reshape((shards,) + out_ref.shape[1:])


def split_arguments(contexts, cotangents, shards):
    cols, tokens = contexts[0].shape
    dtype = contexts[0].dtype
    return pl.pallas_call(
        split_kernel,
        in_specs=[pl.BlockSpec(memory_space=pltpu.VMEM)] * 4,
        out_specs=[pl.BlockSpec(memory_space=pltpu.VMEM)] * 2,
        out_shape=[
            jax.ShapeDtypeStruct((2 * cols, tokens), dtype),
            jax.ShapeDtypeStruct((2 * shards, tokens // shards, cols), dtype),
        ],
    )(*contexts, *cotangents)


def join_kernel(got_ref, out_ref):
    shards, tok, width = out_ref.shape
    main = 2 * MAIN
    sides = [
        got_ref[c * shards : (c + 1) * shards].reshape(shards * tok, width // 2) for c in range(2)
    ]
    for c in range(2):
        out_ref[:, :, c * main : (c + 1) * main] = sides[c][:, :main].reshape(shards, tok, main)
    edges = jnp.concatenate([side[:, main:] for side in sides], axis=1)
    out_ref[:, :, 2 * main :] = edges.reshape(shards, tok, width - 2 * main)


def join_cores(got):
    both, tok, cols = got.shape
    return pl.pallas_call(
        join_kernel,
        in_specs=[pl.BlockSpec(memory_space=pltpu.VMEM)],
        out_specs=pl.BlockSpec(memory_space=pltpu.VMEM),
        out_shape=jax.ShapeDtypeStruct((both // 2, tok, 2 * cols), got.dtype),
    )(got)


def shards(context_one, cotangent_one, context_two, cotangent_two):
    tokens, feats = context_one.shape
    reps = lax.axis_size("replica")
    n_shards = lax.axis_size("shard")
    cols = feats // 2
    same_core = [list(range(c, reps, 2)) for c in range(2)]
    axes = ("replica", "shard")
    size = 2 * n_shards
    planes = [list(range(z * size, (z + 1) * size)) for z in range(reps // 2)]

    ctx, cot = split_arguments(
        (context_one.T, context_two.T), (cotangent_one.T, cotangent_two.T), n_shards
    )
    ctx = lax.all_gather(ctx, "replica")
    cot = join_cores(lax.all_to_all(cot, axes, 0, 0, axis_index_groups=planes))
    cot = lax.all_to_all(cot, "replica", 0, 0, axis_index_groups=same_core)
    pieces = gather_pieces(cot, reps)

    offsets = piece_offsets(tokens // n_shards)
    grads, gram = gradients(ctx, pieces, offsets, tokens)
    gram = jnp.broadcast_to(gram[None], (size,) + gram.shape)
    gram = jnp.sum(lax.all_to_all(gram, axes, 0, 0, axis_index_groups=planes), axis=0)
    gram = jnp.broadcast_to(gram[None], (reps // 2,) + gram.shape)
    gram = lax.all_to_all(gram, "replica", 0, 0, axis_index_groups=same_core)
    one, two = combine(gram, grads, feats, cols, 1.0 / tokens)
    return one.T, two.T


def solution(mesh):
    spec = P("replica", "shard")
    return jax.shard_map(
        shards,
        mesh=mesh,
        in_specs=(spec, spec, spec, spec),
        out_specs=(P("shard", "replica"), P("shard", "replica")),
        check_vma=False,
    )
```

```python
import functools

import jax
import jax.numpy as jnp
import numpy as np
from jax import lax
from jax.experimental import pallas as pl
from jax.experimental.pallas import tpu as pltpu
from jax.sharding import PartitionSpec as P

EPSILON = 1e-06
SIDE = 4
MAIN = 128
SHIFTS = (0, 1, -1, 2)


def plane_moves(reps, stage, d):
    moves = []
    for r in range(reps):
        for y in range(SIDE):
            for x in range(SIDE):
                if (r + stage) % 2:
                    to = y * SIDE + (x + d) % SIDE
                else:
                    to = ((y + d) % SIDE) * SIDE + x
                moves.append((r * SIDE * SIDE + y * SIDE + x, r * SIDE * SIDE + to))
    return moves


def gather_pieces(piece, reps):
    def move(value, stage, d):
        return lax.ppermute(value, ("replica", "shard"), plane_moves(reps, stage, d))

    after, before, far = [move(piece, 0, d) for d in SHIFTS[1:]]
    low, high = jnp.stack([piece, after]), jnp.stack([before, far])
    low_after = move(low, 1, 1)
    high_before = move(high, 1, -1)
    low_before = move(low, 1, -1)
    high_after = move(high, 1, 1)
    low_far = move(low_after, 1, 1)
    high_far = move(high_before, 1, -1)
    return [low, high, low_after, high_after, low_before, high_before, low_far, high_far]


def piece_offsets(tokens_piece):
    me = lax.axis_index("shard")
    core = lax.axis_index("replica") % 2
    y, x = me // SIDE, me % SIDE
    d = jnp.array(SHIFTS, jnp.int32)
    first, second = d[None, :], d[:, None]
    off_0 = ((y - second) % SIDE) * SIDE + (x - first) % SIDE
    off_1 = ((y - first) % SIDE) * SIDE + (x - second) % SIDE
    off = jnp.where(core == 1, off_0, off_1)
    return (off * tokens_piece).astype(jnp.int32).reshape(-1)


def gradient_kernel(off_ref, ctx_hbm, *refs):
    pieces = refs[:8]
    grad_hbm, gram_ref, ctx_ref, cot_ref, grad_ref, acc_ref, ctx_sems, cot_sems, grad_sems = refs[8:]
    chips, _, _, rows, tokens = ctx_hbm.shape
    _, _, tok, width = pieces[0].shape
    reps = 2 * chips
    rem = (width - 4 * MAIN) // 4
    fold = MAIN // rem
    low = rows // fold
    groups = cot_sems.shape[0]
    span = chips // groups

    def ctx_copy(chip):
        return pltpu.make_async_copy(ctx_hbm.at[chip], ctx_ref.at[chip], ctx_sems.at[chip])

    def cot_copy(group, second, first):
        off = pl.multiple_of(off_ref[second * 4 + first], tok)
        part = pl.ds(group * span, span)
        return pltpu.make_async_copy(
            pieces[second * 2 + first // 2].at[first % 2, part],
            cot_ref.at[part, pl.ds(off, tok), :],
            cot_sems.at[group, second, first],
        )

    def grad_copy(chip):
        part = pl.ds(chip * 2, 2)
        return pltpu.make_async_copy(
            grad_ref.at[:, part], grad_hbm.at[:, part], grad_sems.at[chip]
        )

    for group in range(groups):
        for second in range(4):
            for first in range(4):
                cot_copy(group, second, first).start()
        for chip in range(group * span, (group + 1) * span):
            ctx_copy(chip).start()

    quarter = lax.broadcasted_iota(jnp.int32, (low, MAIN), 1) // rem

    def one_chip(chip, carry):
        ctx_copy(chip).wait()
        edge = cot_ref[chip, :, 4 * MAIN :]
        for core in range(2):
            for layer in range(2):
                j = 2 * core + layer
                rhs = jnp.concatenate([cot_ref[chip, :, j * MAIN : (j + 1) * MAIN], edge], axis=1)
                g = jnp.dot(ctx_ref[chip, core, layer], rhs, preferred_element_type=jnp.float32)
                packed = None
                for q in range(fold):
                    part = g[q * low : (q + 1) * low, MAIN:]
                    if (q - j) % fold:
                        part = pltpu.roll(part, ((q - j) % fold) * rem, 1)
                    packed = part if packed is None else jnp.where(quarter == q, part, packed)
                for at, size, value in ((0, rows, g[:, :MAIN]), (rows, low, packed)):
                    grad_ref[layer, chip * 2 + core, at : at + size] = value.astype(jnp.bfloat16)
        grad_copy(chip).start()
        return carry

    for group in range(groups):
        for second in range(4):
            for first in range(4):
                cot_copy(group, second, first).wait()
        lax.fori_loop(group * span, (group + 1) * span, one_chip, 0)

    size = reps * 8
    deep = 25
    acc_ref[...] = jnp.zeros_like(acc_ref)

    def body(i, carry):
        for layer in range(2):
            parts = []
            for u in range(deep):
                at = pl.multiple_of((i * deep + u) * 16, 16)
                part = grad_ref[layer, :, pl.ds(at, 16), :].astype(jnp.float32)
                part = part.reshape(reps, 2, 8, MAIN)
                for h in range(2):
                    parts.append(part[:, h].reshape(size, MAIN).astype(jnp.bfloat16))
            part = jnp.concatenate(parts, axis=1)
            acc_ref[layer] += lax.dot_general(
                part, part, (((1,), (1,)), ((), ())), preferred_element_type=jnp.float32
            )
        return carry

    lax.fori_loop(0, (rows + low) // (16 * deep), body, 0)
    ri = lax.broadcasted_iota(jnp.int32, (size, size), 0)
    ci = lax.broadcasted_iota(jnp.int32, (size, size), 1)
    si = lax.broadcasted_iota(jnp.int32, (size, MAIN), 0)
    sj = lax.broadcasted_iota(jnp.int32, (size, MAIN), 1)
    rows_of = []
    for layer in range(2):
        z = jnp.where(ri % 8 == ci % 8, acc_ref[layer], 0.0)
        rows_of.append(jnp.sum(z.reshape(reps, 8, size), axis=1))
    pick = jnp.where(sj % 32 == si // 8, 1.0, 0.0)
    z = jnp.dot(
        jnp.concatenate(rows_of, axis=0),
        pick,
        precision=lax.Precision.HIGHEST,
        preferred_element_type=jnp.float32,
    )
    place = lax.broadcasted_iota(jnp.int32, (16, MAIN), 1) // 32
    total = z[:16]
    for k in range(1, 4):
        total = jnp.where(place == k, z[16 * k : 16 * (k + 1)], total)
    gram_ref[...] = total
    for chip in range(chips):
        grad_copy(chip).wait()


def gradients(ctx, pieces, offsets, tokens):
    reps, rows2, _ = ctx.shape
    rows = rows2 // 2
    rem = (pieces[0].shape[-1] - 4 * MAIN) // 4
    _, chips, tok, width = pieces[0].shape
    held = rows + rows * rem // MAIN
    groups = 4
    ctx = ctx.reshape(chips, 2, 2, rows, tokens)
    return pl.pallas_call(
        gradient_kernel,
        in_specs=[pl.BlockSpec(memory_space=pltpu.SMEM)] + [pl.BlockSpec(memory_space=pltpu.HBM)] * 9,
        out_specs=[pl.BlockSpec(memory_space=pltpu.HBM), pl.BlockSpec(memory_space=pltpu.VMEM)],
        scratch_shapes=[
            pltpu.VMEM((chips, 2, 2, rows, tokens), jnp.bfloat16),
            pltpu.VMEM((chips, tokens, width), jnp.bfloat16),
            pltpu.VMEM((2, reps, held, MAIN), jnp.bfloat16),
            pltpu.VMEM((2, reps * 8, reps * 8), jnp.float32),
            pltpu.SemaphoreType.DMA((chips,)),
            pltpu.SemaphoreType.DMA((groups, 4, 4)),
            pltpu.SemaphoreType.DMA((chips,)),
        ],
        out_shape=[
            jax.ShapeDtypeStruct((2, reps, held, MAIN), jnp.bfloat16),
            jax.ShapeDtypeStruct((16, MAIN), jnp.float32),
        ],
        compiler_params=pltpu.CompilerParams(vmem_limit_bytes=48 * 1024 * 1024),
    )(offsets, ctx, *pieces)


def tree_weights(gram):
    n = gram.shape[0]
    ri = lax.broadcasted_iota(jnp.int32, (n, n), 0)
    ci = lax.broadcasted_iota(jnp.int32, (n, n), 1)
    weight = jnp.ones((n, 1), jnp.float32)
    for k in range(n.bit_length() - 1):
        same = (ri >> k) == (ci >> k)
        other = (ri >> k) == ((ci >> k) ^ 1)
        twin = ri == (ci ^ (1 << k))
        own = jnp.where(same, gram, 0.0)
        cross = jnp.where(other, gram, 0.0)
        coeffs = []
        for axis in (1, 0):
            norm = jnp.sum(own, axis=1 - axis, keepdims=True)
            norm = jnp.sum(jnp.where(same, norm, 0.0), axis=axis, keepdims=True)
            inner = jnp.sum(cross, axis=1 - axis, keepdims=True)
            inner = jnp.sum(jnp.where(same, inner, 0.0), axis=axis, keepdims=True)
            coeffs.append((jnp.maximum(norm, 0.0), inner))
        (norm_r, inner_r), (norm_c, inner_c) = coeffs
        twin_r = jnp.sum(jnp.where(twin, norm_c, 0.0), axis=1, keepdims=True)
        twin_c = jnp.sum(jnp.where(twin, norm_r, 0.0), axis=0, keepdims=True)
        cap_r = jnp.sqrt(norm_r) * jnp.sqrt(twin_r)
        cap_c = jnp.sqrt(norm_c) * jnp.sqrt(twin_c)
        inner_r = jnp.clip(inner_r, -cap_r, cap_r)
        inner_c = jnp.clip(inner_c, -cap_c, cap_c)
        coeff_r = 1.0 - inner_r / (2.0 * (norm_r + EPSILON))
        coeff_c = 1.0 - inner_c / (2.0 * (norm_c + EPSILON))
        weight = weight * coeff_r
        gram = gram * coeff_r * coeff_c
    return weight


def combine_kernel(scale, gram_ref, grad_hbm, one_hbm, two_hbm, *scratch):
    grad_ref, one_ref, two_ref, weight_ref, grad_sems, out_sems = scratch
    _, reps, held, _ = grad_ref.shape
    cols, rows = one_ref.shape
    rem = cols - MAIN
    low = held - rows
    starts = range(0, held, low)

    def grad_copy(layer, k):
        part = pl.ds(k * low, low)
        return pltpu.make_async_copy(
            grad_hbm.at[layer, :, part], grad_ref.at[layer, :, part], grad_sems.at[layer, k]
        )

    for layer in range(2):
        for k in range(len(starts)):
            grad_copy(layer, k).start()
    total = jnp.sum(gram_ref[...], axis=0) * (scale * scale)
    for layer in range(2):
        parts = [total[:, (2 * layer + h) * 32 : (2 * layer + h + 1) * 32] for h in range(2)]
        weights = tree_weights(jnp.concatenate(parts, axis=0))
        weight_ref[layer] = jnp.broadcast_to(weights * scale, (reps, MAIN))
    outs = []
    for layer, (out_ref, out_hbm) in enumerate(((one_ref, one_hbm), (two_ref, two_hbm))):
        sums = []
        for k, at in enumerate(starts):
            grad_copy(layer, k).wait()
            acc = jnp.zeros((low, MAIN), jnp.float32)
            for r in range(reps):
                value = grad_ref[layer, r, at : at + low].astype(jnp.float32)
                acc += weight_ref[layer, r : r + 1, :] * value
            sums.append(acc)
        out_ref[:MAIN] = jnp.concatenate(sums[:-1], axis=0).T
        edge = sums[-1].T
        for q in range(MAIN // rem):
            out_ref[MAIN:, q * low : (q + 1) * low] = edge[q * rem : (q + 1) * rem]
        outs.append(pltpu.make_async_copy(out_ref, out_hbm, out_sems.at[layer]))
        outs[-1].start()
    for out in outs:
        out.wait()


def combine(gram_parts, grads, rows, cols, scale):
    out = pltpu.HBM((cols, rows), jnp.float32)
    grads = pltpu.with_memory_space_constraint(grads, pltpu.HBM)
    held = grads.shape[2]
    return pl.pallas_call(
        functools.partial(combine_kernel, scale),
        in_specs=[pl.BlockSpec(memory_space=pltpu.VMEM), pl.BlockSpec(memory_space=pltpu.HBM)],
        out_specs=[pl.BlockSpec(memory_space=pltpu.HBM)] * 2,
        out_shape=[out] * 2,
        scratch_shapes=[
            pltpu.VMEM(grads.shape, grads.dtype),
            pltpu.VMEM((cols, rows), jnp.float32),
            pltpu.VMEM((cols, rows), jnp.float32),
            pltpu.VMEM((2, grads.shape[1], MAIN), jnp.float32),
            pltpu.SemaphoreType.DMA((2, held // (held - rows))),
            pltpu.SemaphoreType.DMA((2,)),
        ],
        compiler_params=pltpu.CompilerParams(vmem_limit_bytes=32 * 1024 * 1024),
    )(gram_parts, grads)


def split_kernel(a_ref, b_ref, one_ref, two_ref, ctx_ref, out_ref):
    rows = a_ref.shape[0]
    cols = rows // 2
    shards = out_ref.shape[0] // 2
    ctx_ref[:rows] = a_ref[...]
    ctx_ref[rows:] = b_ref[...]
    both = (one_ref, two_ref)
    for core in range(2):
        at = core * cols
        parts = [ref[at : at + MAIN] for ref in both] + [ref[at + MAIN : at + cols] for ref in both]
        value = jnp.concatenate(parts, axis=0).T
        out_ref[core * shards : (core + 1) * shards] = value.reshape((shards,) + out_ref.shape[1:])


def split_arguments(contexts, cotangents, shards):
    cols, tokens = contexts[0].shape
    dtype = contexts[0].dtype
    return pl.pallas_call(
        split_kernel,
        in_specs=[pl.BlockSpec(memory_space=pltpu.VMEM)] * 4,
        out_specs=[pl.BlockSpec(memory_space=pltpu.VMEM)] * 2,
        out_shape=[
            jax.ShapeDtypeStruct((2 * cols, tokens), dtype),
            jax.ShapeDtypeStruct((2 * shards, tokens // shards, cols), dtype),
        ],
    )(*contexts, *cotangents)


def shards(context_one, cotangent_one, context_two, cotangent_two):
    tokens, feats = context_one.shape
    reps = lax.axis_size("replica")
    n_shards = lax.axis_size("shard")
    cols = feats // 2
    same_core = [list(range(c, reps, 2)) for c in range(2)]
    axes = ("replica", "shard")
    size = 2 * n_shards
    planes = [list(range(z * size, (z + 1) * size)) for z in range(reps // 2)]

    ctx, cot = split_arguments(
        (context_one.T, context_two.T), (cotangent_one.T, cotangent_two.T), n_shards
    )
    ctx = lax.all_gather(ctx, "replica")
    got = lax.all_to_all(cot, axes, 0, 0, axis_index_groups=planes)
    sides = (got[:n_shards], got[n_shards:])
    main = 2 * MAIN
    cot = jnp.concatenate(
        [side[:, :, :main] for side in sides] + [side[:, :, main:] for side in sides], axis=2
    )
    cot = lax.all_to_all(cot, "replica", 0, 0, axis_index_groups=same_core)
    pieces = gather_pieces(cot, reps)

    offsets = piece_offsets(tokens // n_shards)
    grads, gram = gradients(ctx, pieces, offsets, tokens)
    gram = jnp.broadcast_to(gram[None], (size,) + gram.shape)
    gram = jnp.sum(lax.all_to_all(gram, axes, 0, 0, axis_index_groups=planes), axis=0)
    gram = jnp.broadcast_to(gram[None], (reps // 2,) + gram.shape)
    gram = lax.all_to_all(gram, "replica", 0, 0, axis_index_groups=same_core)
    one, two = combine(gram, grads, feats, cols, 1.0 / tokens)
    return one.T, two.T


def solution(mesh):
    spec = P("replica", "shard")
    return jax.shard_map(
        shards,
        mesh=mesh,
        in_specs=(spec, spec, spec, spec),
        out_specs=(P("shard", "replica"), P("shard", "replica")),
        check_vma=False,
    )
```

```python
import functools

import jax
import jax.numpy as jnp
import numpy as np
from jax import lax
from jax.experimental import pallas as pl
from jax.experimental.pallas import tpu as pltpu
from jax.sharding import PartitionSpec as P

EPSILON = 1e-06
SIDE = 4
MAIN = 128
SHIFTS = (0, 1, -1, 2)


def plane_moves(reps, stage, d):
    moves = []
    for r in range(reps):
        for y in range(SIDE):
            for x in range(SIDE):
                if (r + stage) % 2:
                    to = y * SIDE + (x + d) % SIDE
                else:
                    to = ((y + d) % SIDE) * SIDE + x
                moves.append((r * SIDE * SIDE + y * SIDE + x, r * SIDE * SIDE + to))
    return moves


def gather_pieces(piece, reps):
    def move(value, stage, d):
        return lax.ppermute(value, ("replica", "shard"), plane_moves(reps, stage, d))

    after, before, far = [move(piece, 0, d) for d in SHIFTS[1:]]
    low, high = jnp.stack([piece, after]), jnp.stack([before, far])
    low_after = move(low, 1, 1)
    high_before = move(high, 1, -1)
    low_before = move(low, 1, -1)
    high_after = move(high, 1, 1)
    low_far = move(low_after, 1, 1)
    high_far = move(high_before, 1, -1)
    return [low, high, low_after, high_after, low_before, high_before, low_far, high_far]


def piece_offsets(tokens_piece):
    me = lax.axis_index("shard")
    core = lax.axis_index("replica") % 2
    y, x = me // SIDE, me % SIDE
    d = jnp.array(SHIFTS, jnp.int32)
    first, second = d[None, :], d[:, None]
    off_0 = ((y - second) % SIDE) * SIDE + (x - first) % SIDE
    off_1 = ((y - first) % SIDE) * SIDE + (x - second) % SIDE
    off = jnp.where(core == 1, off_0, off_1)
    return (off * tokens_piece).astype(jnp.int32).reshape(-1)


def gradient_kernel(off_ref, ctx_hbm, *refs):
    pieces = refs[:8]
    grad_hbm, gram_ref, ctx_ref, cot_ref, grad_ref, acc_ref, ctx_sems, cot_sems, grad_sems = refs[8:]
    chips, _, _, rows, tokens = ctx_hbm.shape
    _, _, tok, width = pieces[0].shape
    reps = 2 * chips
    rem = (width - 4 * MAIN) // 4
    fold = MAIN // rem
    low = rows // fold
    groups = cot_sems.shape[0]
    span = chips // groups

    def ctx_copy(chip):
        return pltpu.make_async_copy(ctx_hbm.at[chip], ctx_ref.at[chip], ctx_sems.at[chip])

    def cot_copy(group, second, first):
        off = pl.multiple_of(off_ref[second * 4 + first], tok)
        part = pl.ds(group * span, span)
        return pltpu.make_async_copy(
            pieces[second * 2 + first // 2].at[first % 2, part],
            cot_ref.at[part, pl.ds(off, tok), :],
            cot_sems.at[group, second, first],
        )

    def grad_copy(chip):
        part = pl.ds(chip * 2, 2)
        return pltpu.make_async_copy(
            grad_ref.at[:, part], grad_hbm.at[:, part], grad_sems.at[chip]
        )

    for group in range(groups):
        for second in range(4):
            for first in range(4):
                cot_copy(group, second, first).start()
        for chip in range(group * span, (group + 1) * span):
            ctx_copy(chip).start()

    quarter = lax.broadcasted_iota(jnp.int32, (low, MAIN), 1) // rem

    def one_chip(chip, carry):
        ctx_copy(chip).wait()
        edge = cot_ref[chip, :, 4 * MAIN :]
        for core in range(2):
            for layer in range(2):
                j = 2 * core + layer
                rhs = jnp.concatenate([cot_ref[chip, :, j * MAIN : (j + 1) * MAIN], edge], axis=1)
                g = jnp.dot(ctx_ref[chip, core, layer], rhs, preferred_element_type=jnp.float32)
                packed = None
                for q in range(fold):
                    part = g[q * low : (q + 1) * low, MAIN:]
                    if (q - j) % fold:
                        part = pltpu.roll(part, ((q - j) % fold) * rem, 1)
                    packed = part if packed is None else jnp.where(quarter == q, part, packed)
                for at, size, value in ((0, rows, g[:, :MAIN]), (rows, low, packed)):
                    grad_ref[layer, chip * 2 + core, at : at + size] = value.astype(jnp.bfloat16)
        grad_copy(chip).start()
        return carry

    for group in range(groups):
        for second in range(4):
            for first in range(4):
                cot_copy(group, second, first).wait()
        lax.fori_loop(group * span, (group + 1) * span, one_chip, 0)

    size = reps * 8
    deep = 25
    acc_ref[...] = jnp.zeros_like(acc_ref)

    def body(i, carry):
        for layer in range(2):
            parts = []
            for u in range(deep):
                at = pl.multiple_of((i * deep + u) * 16, 16)
                part = grad_ref[layer, :, pl.ds(at, 16), :].astype(jnp.float32)
                part = part.reshape(reps, 2, 8, MAIN)
                for h in range(2):
                    parts.append(part[:, h].reshape(size, MAIN).astype(jnp.bfloat16))
            part = jnp.concatenate(parts, axis=1)
            acc_ref[layer] += lax.dot_general(
                part, part, (((1,), (1,)), ((), ())), preferred_element_type=jnp.float32
            )
        return carry

    lax.fori_loop(0, (rows + low) // (16 * deep), body, 0)
    ri = lax.broadcasted_iota(jnp.int32, (size, size), 0)
    ci = lax.broadcasted_iota(jnp.int32, (size, size), 1)
    si = lax.broadcasted_iota(jnp.int32, (size, MAIN), 0)
    sj = lax.broadcasted_iota(jnp.int32, (size, MAIN), 1)
    rows_of = []
    for layer in range(2):
        z = jnp.where(ri % 8 == ci % 8, acc_ref[layer], 0.0)
        rows_of.append(jnp.sum(z.reshape(reps, 8, size), axis=1))
    pick = jnp.where(sj % 32 == si // 8, 1.0, 0.0)
    z = jnp.dot(
        jnp.concatenate(rows_of, axis=0),
        pick,
        precision=lax.Precision.HIGHEST,
        preferred_element_type=jnp.float32,
    )
    place = lax.broadcasted_iota(jnp.int32, (16, MAIN), 1) // 32
    total = z[:16]
    for k in range(1, 4):
        total = jnp.where(place == k, z[16 * k : 16 * (k + 1)], total)
    gram_ref[...] = total
    for chip in range(chips):
        grad_copy(chip).wait()


def gradients(ctx, pieces, offsets, tokens):
    reps, rows2, _ = ctx.shape
    rows = rows2 // 2
    rem = (pieces[0].shape[-1] - 4 * MAIN) // 4
    _, chips, tok, width = pieces[0].shape
    held = rows + rows * rem // MAIN
    groups = 4
    ctx = ctx.reshape(chips, 2, 2, rows, tokens)
    return pl.pallas_call(
        gradient_kernel,
        in_specs=[pl.BlockSpec(memory_space=pltpu.SMEM)] + [pl.BlockSpec(memory_space=pltpu.HBM)] * 9,
        out_specs=[pl.BlockSpec(memory_space=pltpu.HBM), pl.BlockSpec(memory_space=pltpu.VMEM)],
        scratch_shapes=[
            pltpu.VMEM((chips, 2, 2, rows, tokens), jnp.bfloat16),
            pltpu.VMEM((chips, tokens, width), jnp.bfloat16),
            pltpu.VMEM((2, reps, held, MAIN), jnp.bfloat16),
            pltpu.VMEM((2, reps * 8, reps * 8), jnp.float32),
            pltpu.SemaphoreType.DMA((chips,)),
            pltpu.SemaphoreType.DMA((groups, 4, 4)),
            pltpu.SemaphoreType.DMA((chips,)),
        ],
        out_shape=[
            jax.ShapeDtypeStruct((2, reps, held, MAIN), jnp.bfloat16),
            jax.ShapeDtypeStruct((16, MAIN), jnp.float32),
        ],
        compiler_params=pltpu.CompilerParams(vmem_limit_bytes=48 * 1024 * 1024),
    )(offsets, ctx, *pieces)


def tree_weights(gram):
    n = gram.shape[1]
    ri = lax.broadcasted_iota(jnp.int32, gram.shape, 1)
    ci = lax.broadcasted_iota(jnp.int32, gram.shape, 2)
    weight = jnp.ones((gram.shape[0], n, 1), jnp.float32)
    for k in range(n.bit_length() - 1):
        same = (ri >> k) == (ci >> k)
        other = (ri >> k) == ((ci >> k) ^ 1)
        twin = ri == (ci ^ (1 << k))
        own = jnp.where(same, gram, 0.0)
        cross = jnp.where(other, gram, 0.0)
        coeffs = []
        for axis in (2, 1):
            norm = jnp.sum(own, axis=3 - axis, keepdims=True)
            norm = jnp.sum(jnp.where(same, norm, 0.0), axis=axis, keepdims=True)
            inner = jnp.sum(cross, axis=3 - axis, keepdims=True)
            inner = jnp.sum(jnp.where(same, inner, 0.0), axis=axis, keepdims=True)
            coeffs.append((jnp.maximum(norm, 0.0), inner))
        (norm_r, inner_r), (norm_c, inner_c) = coeffs
        twin_r = jnp.sum(jnp.where(twin, norm_c, 0.0), axis=2, keepdims=True)
        twin_c = jnp.sum(jnp.where(twin, norm_r, 0.0), axis=1, keepdims=True)
        cap_r = jnp.sqrt(norm_r) * jnp.sqrt(twin_r)
        cap_c = jnp.sqrt(norm_c) * jnp.sqrt(twin_c)
        inner_r = jnp.clip(inner_r, -cap_r, cap_r)
        inner_c = jnp.clip(inner_c, -cap_c, cap_c)
        coeff_r = 1.0 - inner_r / (2.0 * (norm_r + EPSILON))
        coeff_c = 1.0 - inner_c / (2.0 * (norm_c + EPSILON))
        weight = weight * coeff_r
        gram = gram * coeff_r * coeff_c
    return weight


def combine_kernel(scale, gram_ref, grad_hbm, one_hbm, two_hbm, *scratch):
    grad_ref, one_ref, two_ref, weight_ref, grad_sems, out_sems = scratch
    _, reps, held, _ = grad_ref.shape
    cols, rows = one_ref.shape
    rem = cols - MAIN
    low = held - rows
    starts = range(0, held, low)

    def grad_copy(layer, k):
        part = pl.ds(k * low, low)
        return pltpu.make_async_copy(
            grad_hbm.at[layer, :, part], grad_ref.at[layer, :, part], grad_sems.at[layer, k]
        )

    for layer in range(2):
        for k in range(len(starts)):
            grad_copy(layer, k).start()
    total = jnp.sum(gram_ref[...], axis=0) * (scale * scale)
    parts = [total[:, k * 32 : (k + 1) * 32] for k in range(4)]
    weights = tree_weights(jnp.concatenate(parts, axis=0).reshape(2, reps, reps))
    for layer in range(2):
        weight_ref[layer] = jnp.broadcast_to(weights[layer] * scale, (reps, MAIN))
    outs = []
    for layer, (out_ref, out_hbm) in enumerate(((one_ref, one_hbm), (two_ref, two_hbm))):
        sums = []
        for k, at in enumerate(starts):
            grad_copy(layer, k).wait()
            acc = jnp.zeros((low, MAIN), jnp.float32)
            for r in range(reps):
                value = grad_ref[layer, r, at : at + low].astype(jnp.float32)
                acc += weight_ref[layer, r : r + 1, :] * value
            sums.append(acc)
        out_ref[:MAIN] = jnp.concatenate(sums[:-1], axis=0).T
        edge = sums[-1].T
        for q in range(MAIN // rem):
            out_ref[MAIN:, q * low : (q + 1) * low] = edge[q * rem : (q + 1) * rem]
        outs.append(pltpu.make_async_copy(out_ref, out_hbm, out_sems.at[layer]))
        outs[-1].start()
    for out in outs:
        out.wait()


def combine(gram_parts, grads, rows, cols, scale):
    out = pltpu.HBM((cols, rows), jnp.float32)
    grads = pltpu.with_memory_space_constraint(grads, pltpu.HBM)
    held = grads.shape[2]
    return pl.pallas_call(
        functools.partial(combine_kernel, scale),
        in_specs=[pl.BlockSpec(memory_space=pltpu.VMEM), pl.BlockSpec(memory_space=pltpu.HBM)],
        out_specs=[pl.BlockSpec(memory_space=pltpu.HBM)] * 2,
        out_shape=[out] * 2,
        scratch_shapes=[
            pltpu.VMEM(grads.shape, grads.dtype),
            pltpu.VMEM((cols, rows), jnp.float32),
            pltpu.VMEM((cols, rows), jnp.float32),
            pltpu.VMEM((2, grads.shape[1], MAIN), jnp.float32),
            pltpu.SemaphoreType.DMA((2, held // (held - rows))),
            pltpu.SemaphoreType.DMA((2,)),
        ],
        compiler_params=pltpu.CompilerParams(vmem_limit_bytes=32 * 1024 * 1024),
    )(gram_parts, grads)


def split_kernel(a_ref, b_ref, one_ref, two_ref, ctx_ref, out_ref):
    rows = a_ref.shape[0]
    cols = rows // 2
    shards = out_ref.shape[0] // 2
    ctx_ref[:rows] = a_ref[...]
    ctx_ref[rows:] = b_ref[...]
    both = (one_ref, two_ref)
    for core in range(2):
        at = core * cols
        parts = [ref[at : at + MAIN] for ref in both] + [ref[at + MAIN : at + cols] for ref in both]
        value = jnp.concatenate(parts, axis=0).T
        out_ref[core * shards : (core + 1) * shards] = value.reshape((shards,) + out_ref.shape[1:])


def split_arguments(contexts, cotangents, shards):
    cols, tokens = contexts[0].shape
    dtype = contexts[0].dtype
    return pl.pallas_call(
        split_kernel,
        in_specs=[pl.BlockSpec(memory_space=pltpu.VMEM)] * 4,
        out_specs=[pl.BlockSpec(memory_space=pltpu.VMEM)] * 2,
        out_shape=[
            jax.ShapeDtypeStruct((2 * cols, tokens), dtype),
            jax.ShapeDtypeStruct((2 * shards, tokens // shards, cols), dtype),
        ],
    )(*contexts, *cotangents)


def shards(context_one, cotangent_one, context_two, cotangent_two):
    tokens, feats = context_one.shape
    reps = lax.axis_size("replica")
    n_shards = lax.axis_size("shard")
    cols = feats // 2
    same_core = [list(range(c, reps, 2)) for c in range(2)]
    axes = ("replica", "shard")
    size = 2 * n_shards
    planes = [list(range(z * size, (z + 1) * size)) for z in range(reps // 2)]

    ctx, cot = split_arguments(
        (context_one.T, context_two.T), (cotangent_one.T, cotangent_two.T), n_shards
    )
    ctx = lax.all_gather(ctx, "replica")
    got = lax.all_to_all(cot, axes, 0, 0, axis_index_groups=planes)
    sides = (got[:n_shards], got[n_shards:])
    main = 2 * MAIN
    cot = jnp.concatenate(
        [side[:, :, :main] for side in sides] + [side[:, :, main:] for side in sides], axis=2
    )
    cot = lax.all_to_all(cot, "replica", 0, 0, axis_index_groups=same_core)
    pieces = gather_pieces(cot, reps)

    offsets = piece_offsets(tokens // n_shards)
    grads, gram = gradients(ctx, pieces, offsets, tokens)
    gram = jnp.broadcast_to(gram[None], (size,) + gram.shape)
    gram = jnp.sum(lax.all_to_all(gram, axes, 0, 0, axis_index_groups=planes), axis=0)
    gram = jnp.broadcast_to(gram[None], (reps // 2,) + gram.shape)
    gram = lax.all_to_all(gram, "replica", 0, 0, axis_index_groups=same_core)
    one, two = combine(gram, grads, feats, cols, 1.0 / tokens)
    return one.T, two.T


def solution(mesh):
    spec = P("replica", "shard")
    return jax.shard_map(
        shards,
        mesh=mesh,
        in_specs=(spec, spec, spec, spec),
        out_specs=(P("shard", "replica"), P("shard", "replica")),
        check_vma=False,
    )
```
